512 devices in a mesh: seq: 64 (over y_lo, z, x), chan: 8 (over y_hi, core).
Axes of the slice: x: 4, y: 8 (y_hi: 4, y_lo: 2; y = y_hi * 2 + y_lo), z: 8, core: 2. Of those that a mesh axis runs over, the one named last changes fastest.
Arguments:
- gate_acts: bfloat16 [65536, 2048], P('seq', 'chan'), may hold values from -40 to 40
- value_acts: bfloat16 [65536, 2048], P('seq', 'chan'), may hold values from -6 to 6
- kernel: bfloat16 [32, 2048], P('chan'), may hold values from -0.125 to 0.125
- norm_gain: float32 [2048], P('chan'), may hold values from 0.1 to 1.9
- out_grad: bfloat16 [65536, 2048], P('seq', 'chan'), may hold values from -30 to 30
Outputs:
- normed: bfloat16 [65536, 2048], P('seq', 'chan')
- gate_grad: bfloat16 [65536, 2048], P('seq', 'chan')
- value_grad: bfloat16 [65536, 2048], P('seq', 'chan')
- kernel_grad: float32 [32, 2048], P('chan')
- gain_grad: float32 [2048], P('chan')
The draws below stay inside these ranges and needn't reach their ends.
All inputs are finite; a program needn't handle non-finite values.
Results may differ from the reference program's by a relative error of at most 0.0085.
Values may be sent and summed in bfloat16 or wider, within the bound.
A program may use at most 128 MiB of HBM per device.

```python
import math
import jax
import jax.numpy as jnp
from jax import lax

D = 2048
HEAD_DIM = 64
LAG = 1024
TOK_DEV = 1024
HEADS = 32
TOKENS = 65536


def log_scales(scale_key, shape):
    return jnp.exp(jax.random.uniform(scale_key, shape, jnp.float32, 0.0, math.log(10.0)))


def draw_gate_acts(key, part):
    row_key, col_key, val_key = jax.random.split(jax.random.fold_in(key, 11), 3)
    values_raw = jnp.clip(jax.random.normal(val_key, (TOKENS, D), jnp.float32), -4.0, 4.0)
    rise_factor = 3.0
    col_scale = rise_factor ** (jnp.arange(D, dtype=jnp.float32) / D)[None, :] * log_scales(col_key, (1, D))
    row_scale = log_scales(row_key, (TOKENS, 1))
    return jnp.clip(0.1 * values_raw * row_scale * col_scale, -40.0, 40.0).astype(jnp.bfloat16)


def draw_out_grad(key, part):
    row_key, col_key, val_key = jax.random.split(jax.random.fold_in(key, 23), 3)
    values_raw = jnp.clip(jax.random.normal(val_key, (TOKENS, D), jnp.float32), -4.0, 4.0)
    rise_factor = 3.0
    row_scale = rise_factor ** (jnp.arange(TOKENS, dtype=jnp.float32) / TOKENS)[:, None] * log_scales(row_key, (TOKENS, 1))
    col_scale = log_scales(col_key, (1, D))
    return jnp.clip(0.05 * values_raw * row_scale * col_scale, -30.0, 30.0).astype(jnp.bfloat16)


def shard_levels(key, dims, shards, least, top_value):
    def one(dim, shards_of):
        heights = jax.random.uniform(jax.random.fold_in(jax.random.fold_in(key, 6), dim), (shards_of,), jnp.float32, least / len(shards), top_value / len(shards))
        return jnp.repeat(jnp.exp(heights), dims[dim] // shards_of).reshape((-1,) + (1,) * (len(dims) - dim - 1))

    gain = one(*shards[0])
    for cut in shards[1:]:
        gain = gain * one(*cut)
    return gain


def noise(own_key, shape, width, reach, cuts=(), kind=jnp.bfloat16):
    level = shard_levels(own_key, shape, cuts, -0.22, 0.18) if cuts else 1.0
    values = jax.random.normal(own_key, shape, jnp.float32) * width * level
    return jnp.minimum(jnp.maximum(values, -reach), reach).astype(kind)


def setup_inputs(seed: int = 0) -> dict:
    key_of = jax.random.split(jax.random.key(seed), 6)
    return {
        "gate_acts": draw_gate_acts(jax.random.fold_in(key_of[5], 71), 0),
        "value_acts": noise(key_of[1], (TOKENS, D), 1.0, 6.0, ((0, 64), (1, 8))),
        "kernel": noise(key_of[2], (HEADS, 2 * LAG), (2 * LAG) ** -0.5, 0.125, ((0, 8),)),
        "norm_gain": jnp.clip(1.0 + 0.18 * jax.random.normal(key_of[3], (D,), jnp.float32), 0.1, 1.9),
        "out_grad": draw_out_grad(jax.random.fold_in(key_of[5], 71), 0),
    }


def circular(kernel_row, places, fft_size):
    return jnp.zeros((fft_size,), kernel_row.dtype).at[places].set(kernel_row)

def reference(gate_acts, value_acts, kernel, norm_gain, out_grad):
    head_count = D // HEAD_DIM
    fft_size = 1 << (TOKENS + 2 * LAG).bit_length()
    lag_index = jnp.arange(2 * LAG, dtype=jnp.int32) - LAG
    ahead = jnp.mod(lag_index, fft_size).astype(jnp.int32)
    behind = jnp.mod(-lag_index, fft_size).astype(jnp.int32)
    kernel_wide = kernel.astype(jnp.float32)

    def spectrum(head_block):
        return jnp.fft.rfft(jnp.pad(head_block, ((0, fft_size - TOKENS), (0, 0))), axis=0)

    def to_heads(values):
        return values.astype(jnp.float32).reshape(TOKENS, head_count, HEAD_DIM).transpose(1, 0, 2)

    def from_heads(values):
        return values.transpose(1, 0, 2).reshape(TOKENS, D)
    value_heads = to_heads(value_acts)

    def forward_head(pieces):
        kernel_row, head_block = pieces
        taps = jnp.fft.rfft(circular(kernel_row, ahead, fft_size))
        return jnp.fft.irfft(spectrum(head_block) * taps[:, None], n=fft_size, axis=0)[:TOKENS]
    mixed_sum = from_heads(lax.map(forward_head, (kernel_wide, value_heads)))

    def norm_block(pieces):
        gate_block, mixed_block, grad_block = pieces
        hidden = gate_block.astype(jnp.float32) * mixed_block
        squares = lax.optimization_barrier(jnp.sum(hidden * hidden, axis=1))
        scale = lax.rsqrt(squares / D + 1e-06)
        normed = (hidden * scale[:, None] * norm_gain[None, :]).astype(jnp.bfloat16)
        weighted = norm_gain[None, :] * grad_block.astype(jnp.float32)
        inner = lax.optimization_barrier(jnp.sum(weighted * hidden, axis=1))
        hidden_grad = scale[:, None] * (weighted - hidden * (scale * scale * inner / D)[:, None])
        gate_grad = (hidden_grad * mixed_block).astype(jnp.bfloat16)
        mix_grad = (hidden_grad * gate_block.astype(jnp.float32)).astype(jnp.bfloat16)
        gain_part = lax.optimization_barrier(jnp.sum(grad_block.astype(jnp.float32) * hidden * scale[:, None], axis=0))
        return (normed, gate_grad, mix_grad, gain_part)
    block_count = TOKENS // TOK_DEV
    normed, gate_grad, mix_grad, gain_parts = lax.map(norm_block, (gate_acts.reshape(block_count, TOK_DEV, D), mixed_sum.reshape(block_count, TOK_DEV, D), out_grad.reshape(block_count, TOK_DEV, D)))
    normed = normed.reshape(TOKENS, D)
    gate_grad = gate_grad.reshape(TOKENS, D)
    mix_heads = to_heads(mix_grad.reshape(TOKENS, D))

    def backward_head(pieces):
        kernel_row, grad_block, head_block = pieces
        taps = jnp.fft.rfft(circular(kernel_row, behind, fft_size))
        grad_spec = spectrum(grad_block)
        value_part = jnp.fft.irfft(grad_spec * taps[:, None], n=fft_size, axis=0)[:TOKENS]
        cross = jnp.fft.irfft(lax.optimization_barrier(jnp.sum(grad_spec * jnp.conj(spectrum(head_block)), axis=1)), n=fft_size)
        return (value_part, cross[ahead])
    value_parts, kernel_sums = lax.map(backward_head, (kernel_wide, mix_heads, value_heads))
    value_grad = from_heads(value_parts).astype(jnp.bfloat16)
    kernel_grad = kernel_sums / math.sqrt(TOKENS * HEAD_DIM)
    gain_grad = lax.optimization_barrier(jnp.sum(gain_parts, axis=0)) / math.sqrt(TOKENS)
    return (normed, gate_grad, value_grad, kernel_grad, gain_grad)
```

```python
import functools
import math

import jax
import jax.numpy as jnp
from jax import lax
from jax.experimental import pallas as pl
from jax.experimental.pallas import tpu as pltpu
from jax.sharding import PartitionSpec as P

EPS = 1e-06
ROWS = 1024
WIDTH = 256
TILE = 256
HEADS = 4
SLOTS = 9
SPAN = 2432
F32 = jnp.float32
BF16 = jnp.bfloat16
MESH = pl.DeviceIdType.MESH


def tile_at(t):
    return pl.ds(t * TILE, TILE)


def build_band(row, first, band, h):
    wide = jnp.concatenate(
        [jnp.broadcast_to(row, (8, 2048)), jnp.zeros((8, SPAN - 2048), F32)], axis=1
    )
    sub = lax.broadcasted_iota(jnp.int32, (8, SPAN), 0)
    if first:
        wide = pltpu.roll(wide, first, 1)
    for bit in (1, 2, 4):
        wide = jnp.where((sub & bit) != 0, pltpu.roll(wide, bit, 1), wide)
    base = jnp.concatenate([wide, pltpu.roll(wide, 8, 1)], axis=0)
    for g in range(8):
        part = (pltpu.roll(base, 16 * g, 1) if g else base).astype(BF16)
        low = jnp.concatenate([jnp.zeros((16, 128), BF16), part[:, : SPAN - 256]], axis=1)
        for s in range(SLOTS):
            band[h, s, 16 * g : 16 * g + 16, :] = part[:, 256 * s : 256 * s + 256]
            band[h, s, 128 + 16 * g : 144 + 16 * g, :] = low[:, 256 * s : 256 * s + 256]


def swap_halves(x):
    return jnp.concatenate([x[:, 64:], x[:, :64]], axis=1)


def make_pair(ext, pairs, t):
    low = lax.broadcasted_iota(jnp.int32, (TILE, 128), 1) < 64
    for hp in range(2):
        a = ext[tile_at(t), 128 * hp : 128 * hp + 128]
        b = ext[tile_at(t + 1), 128 * hp : 128 * hp + 128]
        pairs[2 * hp, t] = jnp.where(low, a, swap_halves(b))
        pairs[2 * hp + 1, t] = jnp.where(low, swap_halves(a), b)


def add_slots(band, pairs, total, slots, fresh=False):
    def one(h, carry):
        acc = None
        for s in slots:
            right = jnp.concatenate([pairs[h, s], pairs[h, s + 2]], axis=1)
            term = jnp.dot(band[h, s], right, preferred_element_type=F32)
            acc = term if acc is None else acc + term
        total[h] = acc if fresh else total[h] + acc
        return carry

    lax.fori_loop(0, HEADS, one, 0)


def to_rows(total, out, dtype):
    low = lax.broadcasted_iota(jnp.int32, (TILE, 128), 1) < 64
    for hp in range(2):
        for pp in range(2):
            a = total[2 * hp, :, 128 * pp : 128 * pp + 128]
            b = total[2 * hp + 1, :, 128 * pp : 128 * pp + 128]
            lanes = slice(128 * hp, 128 * hp + 128)
            out[tile_at(2 * pp), lanes] = jnp.where(low, a, swap_halves(b)).astype(dtype)
            out[tile_at(2 * pp + 1), lanes] = jnp.where(low, swap_halves(a), b).astype(dtype)


def kernel_body(
    dims,
    chans,
    gate_in,
    value_in,
    taps_ref,
    gain_ref,
    grad_in,
    normed_out,
    gate_grad_out,
    value_grad_out,
    taps_grad_ref,
    gain_grad_ref,
    vext,
    mext,
    gate_ref,
    grad_ref,
    ahead,
    behind,
    vpairs,
    mpairs,
    total,
    mixed,
    normed_ref,
    gate_grad_ref,
    value_grad_ref,
    lag_sum,
    chan_buf,
    row_scale,
    gain_sum,
    cut_src,
    cut_buf,
    all_buf,
    gather_buf,
    load_sem,
    store_sem,
    vsend,
    vrecv,
    msend,
    mrecv,
    chan_send,
    chan_recv,
    cut_send,
    cut_recv,
    all_send,
    all_recv,
    gather_send,
    gather_recv,
):
    ny, nz, nx = dims
    nseq = ny * nz * nx
    nq = ny * nx
    cut = 64 // nz
    depth = WIDTH * chans
    me = lax.axis_index("seq")
    ch = lax.axis_index("chan")
    x = lax.rem(me, nx)
    z = lax.rem(lax.div(me, nx), nz)
    y = lax.div(me, nx * nz)
    q = y * nx + x
    has_prev = me > 0
    has_next = me < nseq - 1
    prev_dev = (lax.rem(me + nseq - 1, nseq), ch)
    next_dev = (lax.rem(me + 1, nseq), ch)

    def chan_dev(j):
        return (me, lax.rem(ch + j, chans))

    def z_of(j):
        return lax.rem(z + j, nz)

    def z_dev(j):
        return ((y * nz + z_of(j)) * nx + x, ch)

    def q_dev(j):
        other = lax.rem(q + j, nq)
        return ((lax.div(other, nx) * nz + z) * nx + lax.rem(other, nx), ch)

    barrier = pltpu.get_barrier_semaphore()
    partners = (
        [prev_dev, next_dev]
        + [chan_dev(j) for j in range(1, chans)]
        + [z_dev(j) for j in range(1, nz)]
        + [q_dev(j) for j in range(1, nq)]
    )
    for dev in partners:
        pl.semaphore_signal(barrier, inc=1, device_id=dev, device_id_type=MESH)

    loads = [
        pltpu.make_async_copy(value_in, vext.at[pl.ds(ROWS, ROWS)], load_sem.at[0]),
        pltpu.make_async_copy(gate_in, gate_ref, load_sem.at[1]),
        pltpu.make_async_copy(grad_in, grad_ref, load_sem.at[2]),
    ]
    for load in loads:
        load.start()
    pl.semaphore_wait(barrier, len(partners))

    def to_next(src, ext, send, recv, t):
        return pltpu.make_async_remote_copy(
            src_ref=src,
            dst_ref=ext.at[tile_at(t)],
            send_sem=send.at[0, t],
            recv_sem=recv.at[0, t],
            device_id=next_dev,
            device_id_type=MESH,
        )

    def to_prev(src, ext, send, recv, t):
        return pltpu.make_async_remote_copy(
            src_ref=src,
            dst_ref=ext.at[tile_at(8 + t)],
            send_sem=send.at[1, t],
            recv_sem=recv.at[1, t],
            device_id=prev_dev,
            device_id_type=MESH,
        )

    v_next = [to_next(value_in.at[tile_at(t)], vext, vsend, vrecv, t) for t in range(4)]
    v_prev = [to_prev(value_in.at[tile_at(t)], vext, vsend, vrecv, t) for t in range(4)]
    m_next = [to_next(mext.at[tile_at(4 + t)], mext, msend, mrecv, t) for t in range(4)]
    m_prev = [to_prev(mext.at[tile_at(4 + t)], mext, msend, mrecv, t) for t in range(4)]

    @pl.when(has_next)
    def _():
        for t in (3, 2, 1, 0):
            v_next[t].start()

    @pl.when(has_prev)
    def _():
        for t in range(4):
            v_prev[t].start()

    @pl.when(jnp.logical_not(has_prev))
    def _():
        vext[0:ROWS, :] = jnp.zeros((ROWS, WIDTH), BF16)
        mext[0:ROWS, :] = jnp.zeros((ROWS, WIDTH), BF16)

    @pl.when(jnp.logical_not(has_next))
    def _():
        vext[2 * ROWS : 3 * ROWS, :] = jnp.zeros((ROWS, WIDTH), BF16)
        mext[2 * ROWS : 3 * ROWS, :] = jnp.zeros((ROWS, WIDTH), BF16)

    taps = jnp.concatenate([taps_ref[...].astype(F32), jnp.zeros((4, 2048), F32)], axis=0)
    stacked = jnp.concatenate([taps[:, 128 * b : 128 * b + 128] for b in range(16)], axis=0)
    flip = (
        lax.broadcasted_iota(jnp.int32, (128, 128), 0)
        + lax.broadcasted_iota(jnp.int32, (128, 128), 1)
        == 127
    ).astype(BF16)
    turned = jnp.dot(stacked.astype(BF16), flip, preferred_element_type=F32)
    back = jnp.concatenate([turned[8 * b : 8 * b + 8] for b in reversed(range(16))], axis=1)
    for h in range(HEADS):
        build_band(back[h : h + 1], 1, ahead, h)
    loads[0].wait()
    for t in (4, 5, 6):
        make_pair(vext, vpairs, t)
    add_slots(ahead, vpairs, total, [4], fresh=True)
    for h in range(HEADS):
        build_band(taps[h : h + 1], 0, behind, h)

    def arrive(ext, pairs, band, nexts, prevs, c):
        @pl.when(has_prev)
        def _():
            nexts[4 - c].wait_recv()

        @pl.when(has_next)
        def _():
            prevs[c - 1].wait_recv()

        make_pair(ext, pairs, 4 - c)
        make_pair(ext, pairs, 6 + c)
        add_slots(band, pairs, total, [4 - c, 4 + c])

    loads[1].wait()
    loads[2].wait()
    for c in range(1, 5):
        arrive(vext, vpairs, ahead, v_next, v_prev, c)
    to_rows(total, mixed, F32)

    gain = gain_ref[...]

    def block_at(b):
        return pl.ds(pl.multiple_of(b * 128, 128), 128)

    def sums(b, carry):
        rows = block_at(b)
        hidden = gate_ref[rows, :].astype(F32) * mixed[rows, :]
        square = hidden * hidden
        inner = gain * grad_ref[rows, :].astype(F32) * hidden
        for k, v in ((0, square), (8, inner)):
            half = (v[:, :128] + v[:, 128:]).T
            chan_buf[ch, pl.ds(k + b, 1), :] = jnp.sum(half, axis=0, keepdims=True)
        return carry

    lax.fori_loop(0, 8, sums, 0)

    def exchange(src_of, dst, send, recv, dev_of, count):
        return [
            pltpu.make_async_remote_copy(
                src_ref=src_of(j),
                dst_ref=dst,
                send_sem=send.at[j],
                recv_sem=recv.at[j],
                device_id=dev_of(j),
                device_id_type=MESH,
            )
            for j in range(1, count)
        ]

    chan_copies = exchange(
        lambda j: chan_buf.at[ch], chan_buf.at[ch], chan_send, chan_recv, chan_dev, chans
    )
    for copy in chan_copies:
        copy.start()
    for copy in chan_copies:
        copy.wait_recv()
    sums_all = chan_buf[0]
    for j in range(1, chans):
        sums_all = sums_all + chan_buf[j]
    scale = lax.rsqrt(sums_all[0:8] / depth + EPS)
    row_scale[0:8, :] = scale
    row_scale[8:16, :] = scale * scale * sums_all[8:16] / depth
    gain_sum[...] = jnp.zeros((8, WIDTH), F32)

    def apply(b, carry):
        rows = block_at(b)

        def column(k):
            tall = jnp.broadcast_to(row_scale[pl.ds(k + b, 1), :], (128, 128)).T
            return jnp.concatenate([tall, tall], axis=1)

        scale = column(0)
        pull = column(8)
        gate = gate_ref[rows, :].astype(F32)
        grad = grad_ref[rows, :].astype(F32)
        mix = mixed[rows, :]
        hidden = gate * mix
        scaled = hidden * scale
        normed_ref[rows, :] = (scaled * gain).astype(BF16)
        hidden_grad = scale * (gain * grad - hidden * pull)
        gate_grad_ref[rows, :] = (hidden_grad * mix).astype(BF16)
        mext[pl.ds(pl.multiple_of(ROWS + b * 128, 128), 128), :] = (hidden_grad * gate).astype(BF16)
        term = grad * scaled
        gain_sum[...] += jnp.sum(term.reshape(16, 8, WIDTH), axis=0)
        return carry

    def apply_tile(t):
        lax.fori_loop(2 * t, 2 * t + 2, apply, 0)

    def send_next(*tiles):
        @pl.when(has_next)
        def _():
            for t in tiles:
                m_next[t].start()

    def send_prev(*tiles):
        @pl.when(has_prev)
        def _():
            for t in tiles:
                m_prev[t].start()

    apply_tile(0)
    send_prev(0)
    apply_tile(3)
    send_next(3)
    apply_tile(1)
    send_prev(1)
    apply_tile(2)
    send_next(2, 1, 0)
    send_prev(2, 3)
    stores = [
        pltpu.make_async_copy(normed_ref, normed_out, store_sem.at[0]),
        pltpu.make_async_copy(gate_grad_ref, gate_grad_out, store_sem.at[1]),
        pltpu.make_async_copy(value_grad_ref, value_grad_out, store_sem.at[2]),
    ]
    stores[0].start()
    stores[1].start()

    for t in (4, 5, 6):
        make_pair(mext, mpairs, t)

    def lag_terms(h, carry):
        lag_sum[...] = jnp.zeros((128, SPAN), F32)
        local = jnp.concatenate([mpairs[h, 4], mpairs[h, 6]], axis=1)
        for s in range(SLOTS):
            window = jnp.concatenate([vpairs[h, s], vpairs[h, s + 2]], axis=1)
            cross = lax.dot_general(
                window, local, (((1,), (1,)), ((), ())), preferred_element_type=F32
            )
            for k in range(2):
                at = (17 - 2 * s - k) * 128
                lag_sum[:, at : at + 256] += cross[128 * k : 128 * k + 128]
        eight = lag_sum[0:8, :]
        for g in range(1, 16):
            eight = eight + pltpu.roll(lag_sum[8 * g : 8 * g + 8, :], SPAN - 8 * g, 1)
        sub = lax.broadcasted_iota(jnp.int32, (8, SPAN), 0)
        for bit in (1, 2, 4):
            eight = jnp.where((sub & bit) != 0, pltpu.roll(eight, SPAN - bit, 1), eight)
        line = jnp.sum(eight, axis=0, keepdims=True)
        for b in range(16):
            row = h * 16 + b
            cut_src[lax.div(row, cut), pl.ds(lax.rem(row, cut), 1), :] = line[
                :, 128 + 128 * b : 256 + 128 * b
            ]
        return carry

    lax.fori_loop(0, HEADS, lag_terms, 0)
    gains = jnp.sum(gain_sum[...], axis=0, keepdims=True)
    gain_rows = jnp.concatenate(
        [gains[:, :128], gains[:, 128:], jnp.zeros((6, 128), F32)], axis=0
    )
    for k in range(nz):
        cut_src[k, cut : cut + 8, :] = gain_rows

    cut_copies = exchange(
        lambda j: cut_src.at[z_of(j)], cut_buf.at[z], cut_send, cut_recv, z_dev, nz
    )
    for copy in cut_copies:
        copy.start()
    cut_buf[z] = cut_src[z]

    add_slots(behind, mpairs, total, [4], fresh=True)
    for copy in cut_copies:
        copy.wait_recv()
    part = cut_buf[0]
    for k in range(1, nz):
        part = part + cut_buf[k]
    all_buf[q] = part
    all_copies = exchange(lambda j: all_buf.at[q], all_buf.at[q], all_send, all_recv, q_dev, nq)
    for copy in all_copies:
        copy.start()
    arrive(mext, mpairs, behind, m_next, m_prev, 1)
    for copy in all_copies:
        copy.wait_recv()
    part = all_buf[0]
    for k in range(1, nq):
        part = part + all_buf[k]
    gather_buf[z] = part[0:cut] * (1.0 / math.sqrt(ROWS * nseq * 64))
    gather_copies = exchange(
        lambda j: gather_buf.at[z], gather_buf.at[z], gather_send, gather_recv, z_dev, nz
    )
    for copy in gather_copies:
        copy.start()
    gains = jnp.concatenate([part[cut : cut + 1], part[cut + 1 : cut + 2]], axis=1)
    gain_grad_ref[...] = gains * (1.0 / math.sqrt(ROWS * nseq))
    for c in (2, 3, 4):
        arrive(mext, mpairs, behind, m_next, m_prev, c)
    to_rows(total, value_grad_ref, BF16)
    stores[2].start()
    for copy in gather_copies:
        copy.wait_recv()
    for row in range(64):
        h, b = divmod(row, 16)
        k, r = divmod(row, cut)
        taps_grad_ref[h : h + 1, 128 * b : 128 * b + 128] = gather_buf[k, r : r + 1, :]

    for copy in chan_copies + cut_copies + all_copies + gather_copies:
        copy.wait_send()

    @pl.when(has_next)
    def _():
        for t in range(4):
            v_next[t].wait_send()
            m_next[t].wait_send()

    @pl.when(has_prev)
    def _():
        for t in range(4):
            v_prev[t].wait_send()
            m_prev[t].wait_send()

    for store in stores:
        store.wait()


def on_device(dims, chans, gate_acts, value_acts, taps, norm_gain, out_grad):
    ny, nz, nx = dims
    nq = ny * nx
    cut = 64 // nz
    block = jax.ShapeDtypeStruct((ROWS, WIDTH), BF16)
    anywhere = pl.BlockSpec(memory_space=pl.ANY)
    vmem = pl.BlockSpec(memory_space=pltpu.VMEM)
    dma = pltpu.SemaphoreType.DMA
    call = pl.pallas_call(
        functools.partial(kernel_body, dims, chans),
        out_shape=(
            block,
            block,
            block,
            jax.ShapeDtypeStruct((HEADS, 2048), F32),
            jax.ShapeDtypeStruct((1, WIDTH), F32),
        ),
        in_specs=[anywhere, anywhere, vmem, vmem, anywhere],
        out_specs=(anywhere, anywhere, anywhere, vmem, vmem),
        scratch_shapes=[
            pltpu.VMEM((3 * ROWS, WIDTH), BF16),
            pltpu.VMEM((3 * ROWS, WIDTH), BF16),
            pltpu.VMEM((ROWS, WIDTH), BF16),
            pltpu.VMEM((ROWS, WIDTH), BF16),
            pltpu.VMEM((HEADS, SLOTS, TILE, TILE), BF16),
            pltpu.VMEM((HEADS, SLOTS, TILE, TILE), BF16),
            pltpu.VMEM((HEADS, 11, TILE, 128), BF16),
            pltpu.VMEM((HEADS, 11, TILE, 128), BF16),
            pltpu.VMEM((HEADS, TILE, TILE), F32),
            pltpu.VMEM((ROWS, WIDTH), F32),
            pltpu.VMEM((ROWS, WIDTH), BF16),
            pltpu.VMEM((ROWS, WIDTH), BF16),
            pltpu.VMEM((ROWS, WIDTH), BF16),
            pltpu.VMEM((128, SPAN), F32),
            pltpu.VMEM((chans, 16, 128), F32),
            pltpu.VMEM((16, 128), F32),
            pltpu.VMEM((8, WIDTH), F32),
            pltpu.VMEM((nz, cut + 8, 128), F32),
            pltpu.VMEM((nz, cut + 8, 128), F32),
            pltpu.VMEM((nq, cut + 8, 128), F32),
            pltpu.VMEM((nz, cut, 128), F32),
            dma((3,)),
            dma((3,)),
            dma((2, 4)),
            dma((2, 4)),
            dma((2, 4)),
            dma((2, 4)),
            dma((chans,)),
            dma((chans,)),
            dma((nz,)),
            dma((nz,)),
            dma((nq,)),
            dma((nq,)),
            dma((nz,)),
            dma((nz,)),
        ],
        compiler_params=pltpu.CompilerParams(
            collective_id=0, has_side_effects=True, vmem_limit_bytes=48 * 1024 * 1024
        ),
        cost_estimate=pl.CostEstimate(
            flops=3_700_000_000, bytes_accessed=6_000_000, transcendentals=1024
        ),
        name="toeplitz_mix",
    )
    normed, gate_grad, value_grad, taps_grad, gain_grad = call(
        gate_acts, value_acts, taps, norm_gain.reshape(1, WIDTH), out_grad
    )
    return normed, gate_grad, value_grad, taps_grad, gain_grad.reshape(WIDTH)


def solution(mesh, dims=(2, 8, 4)):
    placed = (P("seq", "chan"), P("seq", "chan"), P("chan", None), P("chan"), P("seq", "chan"))
    return jax.shard_map(
        functools.partial(on_device, dims, mesh.shape["chan"]),
        mesh=mesh,
        in_specs=placed,
        out_specs=(
            P("seq", "chan"),
            P("seq", "chan"),
            P("seq", "chan"),
            P("chan", None),
            P("chan"),
        ),
        check_vma=False,
    )
```

```python
import functools
import math

import jax
import jax.numpy as jnp
from jax import lax
from jax.experimental import pallas as pl
from jax.experimental.pallas import tpu as pltpu
from jax.sharding import PartitionSpec as P

EPS = 1e-06
ROWS = 1024
WIDTH = 256
TILE = 256
HEADS = 4
SLOTS = 9
SPAN = 2432
F32 = jnp.float32
BF16 = jnp.bfloat16
MESH = pl.DeviceIdType.MESH


def far_first(count):
    return sorted(range(1, count), key=lambda j: -min(j, count - j))


def far_first_xy(nx, ny):
    return sorted(range(1, nx * ny), key=lambda j: -min(j % nx, nx - j % nx))


def tile_at(t):
    return pl.ds(t * TILE, TILE)


def build_band(row, first, band, h):
    wide = jnp.concatenate(
        [jnp.broadcast_to(row, (8, 2048)), jnp.zeros((8, SPAN - 2048), F32)], axis=1
    )
    sub = lax.broadcasted_iota(jnp.int32, (8, SPAN), 0)
    if first:
        wide = pltpu.roll(wide, first, 1)
    for bit in (1, 2, 4):
        wide = jnp.where((sub & bit) != 0, pltpu.roll(wide, bit, 1), wide)
    base = jnp.concatenate([wide, pltpu.roll(wide, 8, 1)], axis=0)
    for g in range(8):
        part = (pltpu.roll(base, 16 * g, 1) if g else base).astype(BF16)
        low = jnp.concatenate([jnp.zeros((16, 128), BF16), part[:, : SPAN - 256]], axis=1)
        for s in range(SLOTS):
            band[h, s, 16 * g : 16 * g + 16, :] = part[:, 256 * s : 256 * s + 256]
            band[h, s, 128 + 16 * g : 144 + 16 * g, :] = low[:, 256 * s : 256 * s + 256]


def swap_halves(x):
    return jnp.concatenate([x[:, 64:], x[:, :64]], axis=1)


def make_pair(ext, pairs, t):
    low = lax.broadcasted_iota(jnp.int32, (TILE, 128), 1) < 64
    for hp in range(2):
        a = ext[tile_at(t), 128 * hp : 128 * hp + 128]
        b = ext[tile_at(t + 1), 128 * hp : 128 * hp + 128]
        pairs[2 * hp, t] = jnp.where(low, a, swap_halves(b))
        pairs[2 * hp + 1, t] = jnp.where(low, swap_halves(a), b)


def add_slots(band, pairs, total, slots, fresh=False):
    def one(h, carry):
        acc = None
        for s in slots:
            right = jnp.concatenate([pairs[h, s], pairs[h, s + 2]], axis=1)
            term = jnp.dot(band[h, s], right, preferred_element_type=F32)
            acc = term if acc is None else acc + term
        total[h] = acc if fresh else total[h] + acc
        return carry

    lax.fori_loop(0, HEADS, one, 0)


def outer_rows(total, put):
    low = lax.broadcasted_iota(jnp.int32, (TILE, 128), 1) < 64
    for hp in range(2):
        a = total[2 * hp, :, 0:128]
        b = total[2 * hp + 1, :, 0:128]
        put(0, hp, jnp.where(low, a, swap_halves(b)))
        a = total[2 * hp, :, 128:256]
        b = total[2 * hp + 1, :, 128:256]
        put(3, hp, jnp.where(low, swap_halves(a), b))


def inner_rows(total, extra, put):
    low = lax.broadcasted_iota(jnp.int32, (TILE, 128), 1) < 64
    for hp in range(2):
        more_a = 0.0 if extra is None else extra[2 * hp]
        more_b = 0.0 if extra is None else extra[2 * hp + 1]
        swap_a = 0.0 if extra is None else swap_halves(more_a)
        swap_b = 0.0 if extra is None else swap_halves(more_b)
        a = total[2 * hp, :, 0:128]
        b = total[2 * hp + 1, :, 0:128]
        put(1, hp, jnp.where(low, swap_halves(a) + more_a, b + swap_b))
        a = total[2 * hp, :, 128:256]
        b = total[2 * hp + 1, :, 128:256]
        put(2, hp, jnp.where(low, a + swap_a, swap_halves(b) + more_b))


def kernel_body(
    dims,
    chans,
    gate_in,
    value_in,
    taps_in,
    gain_in,
    grad_in,
    normed_out,
    gate_grad_out,
    value_grad_out,
    taps_grad_ref,
    gain_grad_ref,
    vext,
    mext,
    gate_ref,
    grad_ref,
    taps_ref,
    gain_ref,
    ahead,
    behind,
    vpairs,
    mpairs,
    total,
    extra,
    mixed,
    lag_sum,
    chan_buf,
    row_scale,
    gain_sum,
    cut_src,
    cut_buf,
    all_buf,
    gather_buf,
    load_sem,
    vsend,
    vrecv,
    msend,
    mrecv,
    chan_send,
    chan_recv,
    cut_send,
    cut_recv,
    all_send,
    all_recv,
    gather_send,
    gather_recv,
):
    ny, nz, nx = dims
    nseq = ny * nz * nx
    nq = ny * nx
    cut = 64 // nz
    depth = WIDTH * chans
    me = lax.axis_index("seq")
    ch = lax.axis_index("chan")
    x = lax.rem(me, nx)
    z = lax.rem(lax.div(me, nx), nz)
    y = lax.div(me, nx * nz)
    q = y * nx + x
    has_prev = me > 0
    has_next = me < nseq - 1
    prev_dev = (lax.rem(me + nseq - 1, nseq), ch)
    next_dev = (lax.rem(me + 1, nseq), ch)

    def chan_dev(j):
        return (me, lax.rem(ch + j, chans))

    def z_of(j):
        return lax.rem(z + j, nz)

    def z_dev(j):
        return ((y * nz + z_of(j)) * nx + x, ch)

    def q_dev(j):
        other = lax.rem(q + j, nq)
        return ((lax.div(other, nx) * nz + z) * nx + lax.rem(other, nx), ch)

    barrier = pltpu.get_barrier_semaphore()
    partners = (
        [z_dev(j) for j in far_first(nz)]
        + [chan_dev(j) for j in far_first(chans)]
        + [q_dev(j) for j in far_first_xy(nx, ny)]
        + [prev_dev, next_dev]
    )
    for dev in partners:
        pl.semaphore_signal(barrier, inc=1, device_id=dev, device_id_type=MESH)

    loads = [
        pltpu.make_async_copy(value_in, vext.at[pl.ds(ROWS, ROWS)], load_sem.at[0]),
        pltpu.make_async_copy(gate_in, gate_ref, load_sem.at[1]),
        pltpu.make_async_copy(grad_in, grad_ref, load_sem.at[2]),
        pltpu.make_async_copy(taps_in, taps_ref, load_sem.at[3]),
        pltpu.make_async_copy(gain_in, gain_ref, load_sem.at[4]),
    ]
    for k in (3, 0, 1, 2, 4):
        loads[k].start()
    pl.semaphore_wait(barrier, len(partners))

    def to_next(src, ext, send, recv, t):
        return pltpu.make_async_remote_copy(
            src_ref=src,
            dst_ref=ext.at[tile_at(t)],
            send_sem=send.at[0, t],
            recv_sem=recv.at[0, t],
            device_id=next_dev,
            device_id_type=MESH,
        )

    def to_prev(src, ext, send, recv, t):
        return pltpu.make_async_remote_copy(
            src_ref=src,
            dst_ref=ext.at[tile_at(8 + t)],
            send_sem=send.at[1, t],
            recv_sem=recv.at[1, t],
            device_id=prev_dev,
            device_id_type=MESH,
        )

    v_next = [to_next(value_in.at[tile_at(t)], vext, vsend, vrecv, t) for t in range(4)]
    v_prev = [to_prev(value_in.at[tile_at(t)], vext, vsend, vrecv, t) for t in range(4)]
    m_next = [to_next(mext.at[tile_at(4 + t)], mext, msend, mrecv, t) for t in range(4)]
    m_prev = [to_prev(mext.at[tile_at(4 + t)], mext, msend, mrecv, t) for t in range(4)]

    @pl.when(has_next)
    def _():
        for t in (3, 2, 1, 0):
            v_next[t].start()

    @pl.when(has_prev)
    def _():
        for t in range(4):
            v_prev[t].start()

    @pl.when(jnp.logical_not(has_prev))
    def _():
        vext[0:ROWS, :] = jnp.zeros((ROWS, WIDTH), BF16)
        mext[0:ROWS, :] = jnp.zeros((ROWS, WIDTH), BF16)

    @pl.when(jnp.logical_not(has_next))
    def _():
        vext[2 * ROWS : 3 * ROWS, :] = jnp.zeros((ROWS, WIDTH), BF16)
        mext[2 * ROWS : 3 * ROWS, :] = jnp.zeros((ROWS, WIDTH), BF16)

    loads[3].wait()
    taps = jnp.concatenate([taps_ref[...].astype(F32), jnp.zeros((4, 2048), F32)], axis=0)
    stacked = jnp.concatenate([taps[:, 128 * b : 128 * b + 128] for b in range(16)], axis=0)
    flip = (
        lax.broadcasted_iota(jnp.int32, (128, 128), 0)
        + lax.broadcasted_iota(jnp.int32, (128, 128), 1)
        == 127
    ).astype(BF16)
    turned = jnp.dot(stacked.astype(BF16), flip, preferred_element_type=F32)
    back = jnp.concatenate([turned[8 * b : 8 * b + 8] for b in reversed(range(16))], axis=1)
    for h in range(HEADS):
        build_band(back[h : h + 1], 1, ahead, h)
    loads[0].wait()
    for t in (4, 5, 6):
        make_pair(vext, vpairs, t)
    add_slots(ahead, vpairs, total, [4], fresh=True)
    for h in range(HEADS):
        build_band(taps[h : h + 1], 0, behind, h)

    def arrive(nexts, prevs, below, above):
        @pl.when(has_prev)
        def _():
            for t in below:
                nexts[t].wait_recv()

        @pl.when(has_next)
        def _():
            for t in above:
                prevs[t].wait_recv()

    def put_mixed(p, hp, block):
        mixed[tile_at(p), 128 * hp : 128 * hp + 128] = block

    for c in (1, 2, 3):
        arrive(v_next, v_prev, [4 - c], [c - 1])
        make_pair(vext, vpairs, 4 - c)
        make_pair(vext, vpairs, 6 + c)
        add_slots(ahead, vpairs, total, [4 - c, 4 + c])

    def between(h, carry):
        extra[h] = jnp.dot(ahead[h, 0], vpairs[h, 1], preferred_element_type=F32) + jnp.dot(
            ahead[h, 8], vpairs[h, 9], preferred_element_type=F32
        )
        return carry

    lax.fori_loop(0, HEADS, between, 0)
    inner_rows(total, extra, put_mixed)
    for k in (1, 2, 4):
        loads[k].wait()

    gain = gain_ref[...]

    def block_at(b):
        return pl.ds(pl.multiple_of(b * 128, 128), 128)

    def sums(stage, b, at):
        rows = block_at(b)
        hidden = gate_ref[rows, :].astype(F32) * mixed[rows, :]
        square = hidden * hidden
        inner = gain * grad_ref[rows, :].astype(F32) * hidden
        for k, v in ((0, square), (4, inner)):
            half = (v[:, :128] + v[:, 128:]).T
            chan_buf[stage, ch, pl.ds(k + at, 1), :] = jnp.sum(half, axis=0, keepdims=True)

    def inner_sums(i, carry):
        sums(0, i + 2, i)
        return carry

    def outer_sums(i, carry):
        sums(1, i + 4 * lax.div(i, 2), i)
        return carry

    def exchange(src_of, dst, send, recv, dev_of, order):
        return [
            pltpu.make_async_remote_copy(
                src_ref=src_of(j),
                dst_ref=dst,
                send_sem=send.at[j],
                recv_sem=recv.at[j],
                device_id=dev_of(j),
                device_id_type=MESH,
            )
            for j in order
        ]

    chan_copies = [
        exchange(
            lambda j, k=k: chan_buf.at[k, ch],
            chan_buf.at[k, ch],
            chan_send.at[k],
            chan_recv.at[k],
            chan_dev,
            far_first(chans),
        )
        for k in range(2)
    ]

    def scales(stage):
        for copy in chan_copies[stage]:
            copy.wait_recv()
        sums_all = chan_buf[stage, 0]
        for j in range(1, chans):
            sums_all = sums_all + chan_buf[stage, j]
        scale = lax.rsqrt(sums_all[0:4] / depth + EPS)
        row_scale[stage, 0:4, :] = scale
        row_scale[stage, 4:8, :] = scale * scale * sums_all[4:8] / depth

    gain_sum[...] = jnp.zeros((8, WIDTH), F32)

    def apply(stage, b, at):
        rows = block_at(b)

        def column(k):
            tall = jnp.broadcast_to(row_scale[stage, pl.ds(k + at, 1), :], (128, 128)).T
            return jnp.concatenate([tall, tall], axis=1)

        scale = column(0)
        pull = column(4)
        gate = gate_ref[rows, :].astype(F32)
        grad = grad_ref[rows, :].astype(F32)
        mix = mixed[rows, :]
        hidden = gate * mix
        scaled = hidden * scale
        normed_out[rows, :] = (scaled * gain).astype(BF16)
        hidden_grad = scale * (gain * grad - hidden * pull)
        gate_grad_out[rows, :] = (hidden_grad * mix).astype(BF16)
        mext[pl.ds(pl.multiple_of(ROWS + b * 128, 128), 128), :] = (hidden_grad * gate).astype(BF16)
        term = grad * scaled
        gain_sum[...] += jnp.sum(term.reshape(16, 8, WIDTH), axis=0)

    def apply_tile(t):
        def one(i, carry):
            if t in (1, 2):
                apply(0, 2 * t + i, 2 * t - 2 + i)
            else:
                apply(1, 2 * t + i, (0 if t == 0 else 2) + i)
            return carry

        lax.fori_loop(0, 2, one, 0)

    def send_next(*tiles):
        @pl.when(has_next)
        def _():
            for t in tiles:
                m_next[t].start()

    def send_prev(*tiles):
        @pl.when(has_prev)
        def _():
            for t in tiles:
                m_prev[t].start()

    lax.fori_loop(0, 4, inner_sums, 0)
    for copy in chan_copies[0]:
        copy.start()
    arrive(v_next, v_prev, [0], [3])
    make_pair(vext, vpairs, 0)
    make_pair(vext, vpairs, 10)
    add_slots(ahead, vpairs, total, [0, 8])
    outer_rows(total, put_mixed)
    lax.fori_loop(0, 4, outer_sums, 0)
    for copy in chan_copies[1]:
        copy.start()
    scales(0)
    apply_tile(1)
    send_prev(1)
    apply_tile(2)
    send_next(2, 1)
    send_prev(2)
    scales(1)
    apply_tile(0)
    send_prev(0)
    apply_tile(3)
    send_next(3)

    for t in (4, 5, 6):
        make_pair(mext, mpairs, t)

    def lag_terms(h, carry):
        local = jnp.concatenate([mpairs[h, 4], mpairs[h, 6]], axis=1)
        for s in range(SLOTS):
            window = jnp.concatenate([vpairs[h, s], vpairs[h, s + 2]], axis=1)
            cross = lax.dot_general(
                window, local, (((1,), (1,)), ((), ())), preferred_element_type=F32
            )
            at = (17 - 2 * s) * 128
            right = cross[0:128, 128:256]
            lag_sum[:, at + 128 : at + 256] = right if s == 0 else right + held
            lag_sum[:, at : at + 128] = cross[0:128, 0:128] + cross[128:256, 128:256]
            held = cross[128:256, 0:128]
        lag_sum[:, 0:128] = held
        eight = lag_sum[0:8, :]
        for g in range(1, 16):
            eight = eight + pltpu.roll(lag_sum[8 * g : 8 * g + 8, :], SPAN - 8 * g, 1)
        sub = lax.broadcasted_iota(jnp.int32, (8, SPAN), 0)
        for bit in (1, 2, 4):
            eight = jnp.where((sub & bit) != 0, pltpu.roll(eight, SPAN - bit, 1), eight)
        line = jnp.sum(eight, axis=0, keepdims=True)
        for b in range(16):
            row = h * 16 + b
            cut_src[lax.div(row, cut), pl.ds(lax.rem(row, cut), 1), :] = line[
                :, 128 + 128 * b : 256 + 128 * b
            ]
        return carry

    lax.fori_loop(0, HEADS, lag_terms, 0)
    gains = jnp.sum(gain_sum[...], axis=0, keepdims=True)
    gain_rows = jnp.concatenate(
        [gains[:, :128], gains[:, 128:], jnp.zeros((6, 128), F32)], axis=0
    )
    for k in range(nz):
        cut_src[k, cut : cut + 8, :] = gain_rows

    cut_copies = exchange(
        lambda j: cut_src.at[z_of(j)], cut_buf.at[z], cut_send, cut_recv, z_dev, far_first(nz)
    )
    for copy in cut_copies:
        copy.start()
    send_next(0)
    send_prev(3)
    cut_buf[z] = cut_src[z]

    add_slots(behind, mpairs, total, [4], fresh=True)
    arrive(m_next, m_prev, [2, 1, 3], [1, 2, 0])
    for t in (1, 2, 3, 7, 8, 9):
        make_pair(mext, mpairs, t)
    add_slots(behind, mpairs, total, [1, 2, 3])
    add_slots(behind, mpairs, total, [5, 6, 7])
    for copy in cut_copies:
        copy.wait_recv()
    part = cut_buf[0]
    for k in range(1, nz):
        part = part + cut_buf[k]
    all_buf[q] = part
    all_copies = exchange(
        lambda j: all_buf.at[q], all_buf.at[q], all_send, all_recv, q_dev, far_first_xy(nx, ny)
    )
    for copy in all_copies:
        copy.start()
    arrive(m_next, m_prev, [0], [3])
    make_pair(mext, mpairs, 0)
    make_pair(mext, mpairs, 10)
    add_slots(behind, mpairs, total, [0, 8])

    def put_grad(p, hp, block):
        value_grad_out[tile_at(p), 128 * hp : 128 * hp + 128] = block.astype(BF16)

    outer_rows(total, put_grad)
    inner_rows(total, None, put_grad)
    for copy in all_copies:
        copy.wait_recv()
    part = all_buf[0]
    for k in range(1, nq):
        part = part + all_buf[k]
    gather_buf[z] = part[0:cut] * (1.0 / math.sqrt(ROWS * nseq * 64))
    gather_copies = exchange(
        lambda j: gather_buf.at[z], gather_buf.at[z], gather_send, gather_recv, z_dev, far_first(nz)
    )
    for copy in gather_copies:
        copy.start()
    gains = jnp.concatenate([part[cut : cut + 1], part[cut + 1 : cut + 2]], axis=1)
    gain_grad_ref[...] = gains * (1.0 / math.sqrt(ROWS * nseq))
    for copy in gather_copies:
        copy.wait_recv()
    for row in range(64):
        h, b = divmod(row, 16)
        k, r = divmod(row, cut)
        taps_grad_ref[h : h + 1, 128 * b : 128 * b + 128] = gather_buf[k, r : r + 1, :]

    for copy in chan_copies[0] + chan_copies[1] + cut_copies + all_copies + gather_copies:
        copy.wait_send()

    @pl.when(has_next)
    def _():
        for t in range(4):
            v_next[t].wait_send()
            m_next[t].wait_send()

    @pl.when(has_prev)
    def _():
        for t in range(4):
            v_prev[t].wait_send()
            m_prev[t].wait_send()


def write_out(*refs):
    sources, targets, sem = refs[:5], refs[5:10], refs[10]
    copies = [
        pltpu.make_async_copy(source, target, sem.at[k])
        for k, (source, target) in enumerate(zip(sources, targets))
    ]
    for copy in copies:
        copy.start()
    for copy in copies:
        copy.wait()


def on_device(dims, chans, gate_acts, value_acts, taps, norm_gain, out_grad):
    ny, nz, nx = dims
    nq = ny * nx
    cut = 64 // nz
    block = jax.ShapeDtypeStruct((ROWS, WIDTH), BF16)
    hbm = pl.BlockSpec(memory_space=pltpu.HBM)
    vmem = pl.BlockSpec(memory_space=pltpu.VMEM)
    dma = pltpu.SemaphoreType.DMA
    call = pl.pallas_call(
        functools.partial(kernel_body, dims, chans),
        out_shape=(
            block,
            block,
            block,
            jax.ShapeDtypeStruct((HEADS, 2048), F32),
            jax.ShapeDtypeStruct((1, WIDTH), F32),
        ),
        in_specs=[hbm] * 5,
        out_specs=(vmem,) * 5,
        scratch_shapes=[
            pltpu.VMEM((3 * ROWS, WIDTH), BF16),
            pltpu.VMEM((3 * ROWS, WIDTH), BF16),
            pltpu.VMEM((ROWS, WIDTH), BF16),
            pltpu.VMEM((ROWS, WIDTH), BF16),
            pltpu.VMEM((HEADS, 2048), BF16),
            pltpu.VMEM((1, WIDTH), F32),
            pltpu.VMEM((HEADS, SLOTS, TILE, TILE), BF16),
            pltpu.VMEM((HEADS, SLOTS, TILE, TILE), BF16),
            pltpu.VMEM((HEADS, 11, TILE, 128), BF16),
            pltpu.VMEM((HEADS, 11, TILE, 128), BF16),
            pltpu.VMEM((HEADS, TILE, TILE), F32),
            pltpu.VMEM((HEADS, TILE, 128), F32),
            pltpu.VMEM((ROWS, WIDTH), F32),
            pltpu.VMEM((128, SPAN), F32),
            pltpu.VMEM((2, chans, 8, 128), F32),
            pltpu.VMEM((2, 8, 128), F32),
            pltpu.VMEM((8, WIDTH), F32),
            pltpu.VMEM((nz, cut + 8, 128), F32),
            pltpu.VMEM((nz, cut + 8, 128), F32),
            pltpu.VMEM((nq, cut + 8, 128), F32),
            pltpu.VMEM((nz, cut, 128), F32),
            dma((5,)),
            dma((2, 4)),
            dma((2, 4)),
            dma((2, 4)),
            dma((2, 4)),
            dma((2, chans)),
            dma((2, chans)),
            dma((nz,)),
            dma((nz,)),
            dma((nq,)),
            dma((nq,)),
            dma((nz,)),
            dma((nz,)),
        ],
        compiler_params=pltpu.CompilerParams(
            collective_id=0, has_side_effects=True, vmem_limit_bytes=52 * 1024 * 1024
        ),
        cost_estimate=pl.CostEstimate(
            flops=3_700_000_000, bytes_accessed=6_000_000, transcendentals=1024
        ),
        name="toeplitz_mix",
    )
    operands = (gate_acts, value_acts, taps, norm_gain.reshape(1, WIDTH), out_grad)
    results = call(*[pltpu.with_memory_space_constraint(v, pltpu.HBM) for v in operands])
    normed, gate_grad, value_grad, taps_grad, gain_grad = pl.pallas_call(
        write_out,
        out_shape=[jax.ShapeDtypeStruct(r.shape, r.dtype) for r in results],
        in_specs=[vmem] * 5,
        out_specs=[hbm] * 5,
        scratch_shapes=[dma((5,))],
        compiler_params=pltpu.CompilerParams(vmem_limit_bytes=8 * 1024 * 1024),
        name="write_out",
    )(*results)
    return normed, gate_grad, value_grad, taps_grad, gain_grad.reshape(WIDTH)


def solution(mesh, dims=(2, 8, 4)):
    placed = (P("seq", "chan"), P("seq", "chan"), P("chan", None), P("chan"), P("seq", "chan"))
    return jax.shard_map(
        functools.partial(on_device, dims, mesh.shape["chan"]),
        mesh=mesh,
        in_specs=placed,
        out_specs=(
            P("seq", "chan"),
            P("seq", "chan"),
            P("seq", "chan"),
            P("chan", None),
            P("chan"),
        ),
        check_vma=False,
    )
```

```python
import functools
import math

import jax
import jax.numpy as jnp
from jax import lax
from jax.experimental import pallas as pl
from jax.experimental.pallas import tpu as pltpu
from jax.sharding import PartitionSpec as P

EPS = 1e-06
ROWS = 1024
WIDTH = 256
TILE = 256
HEADS = 4
SLOTS = 9
SPAN = 2432
F32 = jnp.float32
BF16 = jnp.bfloat16
MESH = pl.DeviceIdType.MESH


def far_first(count):
    return sorted(range(1, count), key=lambda j: -min(j, count - j))


def far_first_xy(nx, ny):
    return sorted(range(1, nx * ny), key=lambda j: -min(j % nx, nx - j % nx))


def tile_at(t):
    return pl.ds(t * TILE, TILE)


def build_band(row, first, band, h):
    wide = jnp.concatenate(
        [jnp.broadcast_to(row, (8, 2048)), jnp.zeros((8, SPAN - 2048), F32)], axis=1
    )
    sub = lax.broadcasted_iota(jnp.int32, (8, SPAN), 0)
    if first:
        wide = pltpu.roll(wide, first, 1)
    for bit in (1, 2, 4):
        wide = jnp.where((sub & bit) != 0, pltpu.roll(wide, bit, 1), wide)
    base = jnp.concatenate([wide, pltpu.roll(wide, 8, 1)], axis=0)
    for g in range(8):
        part = (pltpu.roll(base, 16 * g, 1) if g else base).astype(BF16)
        low = jnp.concatenate([jnp.zeros((16, 128), BF16), part[:, : SPAN - 256]], axis=1)
        for s in range(SLOTS):
            band[h, s, 16 * g : 16 * g + 16, :] = part[:, 256 * s : 256 * s + 256]
            band[h, s, 128 + 16 * g : 144 + 16 * g, :] = low[:, 256 * s : 256 * s + 256]


def swap_halves(x):
    return jnp.concatenate([x[:, 64:], x[:, :64]], axis=1)


def make_pair(ext, pairs, t):
    low = lax.broadcasted_iota(jnp.int32, (TILE, 128), 1) < 64
    for hp in range(2):
        a = ext[tile_at(t), 128 * hp : 128 * hp + 128]
        b = ext[tile_at(t + 1), 128 * hp : 128 * hp + 128]
        pairs[2 * hp, t] = jnp.where(low, a, swap_halves(b))
        pairs[2 * hp + 1, t] = jnp.where(low, swap_halves(a), b)


def add_slots(band, pairs, total, slots, fresh=False):
    def one(h, carry):
        acc = None
        for s in slots:
            right = jnp.concatenate([pairs[h, s], pairs[h, s + 2]], axis=1)
            term = jnp.dot(band[h, s], right, preferred_element_type=F32)
            acc = term if acc is None else acc + term
        total[h] = acc if fresh else total[h] + acc
        return carry

    lax.fori_loop(0, HEADS, one, 0)


def outer_rows(total, put):
    low = lax.broadcasted_iota(jnp.int32, (TILE, 128), 1) < 64
    for hp in range(2):
        a = total[2 * hp, :, 0:128]
        b = total[2 * hp + 1, :, 0:128]
        put(0, hp, jnp.where(low, a, swap_halves(b)))
        a = total[2 * hp, :, 128:256]
        b = total[2 * hp + 1, :, 128:256]
        put(3, hp, jnp.where(low, swap_halves(a), b))


def inner_rows(total, extra, put):
    low = lax.broadcasted_iota(jnp.int32, (TILE, 128), 1) < 64
    for hp in range(2):
        more_a = 0.0 if extra is None else extra[2 * hp]
        more_b = 0.0 if extra is None else extra[2 * hp + 1]
        swap_a = 0.0 if extra is None else swap_halves(more_a)
        swap_b = 0.0 if extra is None else swap_halves(more_b)
        a = total[2 * hp, :, 0:128]
        b = total[2 * hp + 1, :, 0:128]
        put(1, hp, jnp.where(low, swap_halves(a) + more_a, b + swap_b))
        a = total[2 * hp, :, 128:256]
        b = total[2 * hp + 1, :, 128:256]
        put(2, hp, jnp.where(low, a + swap_a, swap_halves(b) + more_b))


def kernel_body(
    dims,
    chans,
    gate_in,
    value_in,
    taps_in,
    gain_in,
    grad_in,
    normed_out,
    gate_grad_out,
    value_grad_out,
    taps_grad_ref,
    gain_grad_ref,
    vext,
    mext,
    gate_ref,
    grad_ref,
    taps_ref,
    gain_ref,
    ahead,
    behind,
    vpairs,
    mpairs,
    total,
    extra,
    mixed,
    lag_sum,
    chan_buf,
    row_scale,
    gain_sum,
    cut_src,
    cut_buf,
    all_buf,
    gather_buf,
    load_sem,
    vsend,
    vrecv,
    msend,
    mrecv,
    chan_send,
    chan_recv,
    cut_send,
    cut_recv,
    all_send,
    all_recv,
    gather_send,
    gather_recv,
):
    ny, nz, nx = dims
    nseq = ny * nz * nx
    nq = ny * nx
    cut = 64 // nz
    depth = WIDTH * chans
    me = lax.axis_index("seq")
    ch = lax.axis_index("chan")
    x = lax.rem(me, nx)
    z = lax.rem(lax.div(me, nx), nz)
    y = lax.div(me, nx * nz)
    q = y * nx + x
    has_prev = me > 0
    has_next = me < nseq - 1
    prev_dev = (lax.rem(me + nseq - 1, nseq), ch)
    next_dev = (lax.rem(me + 1, nseq), ch)

    def chan_dev(j):
        return (me, lax.rem(ch + j, chans))

    def z_of(j):
        return lax.rem(z + j, nz)

    def z_dev(j):
        return ((y * nz + z_of(j)) * nx + x, ch)

    def q_dev(j):
        other = lax.rem(q + j, nq)
        return ((lax.div(other, nx) * nz + z) * nx + lax.rem(other, nx), ch)

    barrier = pltpu.get_barrier_semaphore()
    partners = (
        [prev_dev, next_dev]
        + [z_dev(j) for j in far_first(nz)]
        + [chan_dev(j) for j in far_first(chans)]
        + [q_dev(j) for j in far_first_xy(nx, ny)]
    )
    for dev in partners:
        pl.semaphore_signal(barrier, inc=1, device_id=dev, device_id_type=MESH)

    loads = [
        pltpu.make_async_copy(value_in, vext.at[pl.ds(ROWS, ROWS)], load_sem.at[0]),
        pltpu.make_async_copy(gate_in, gate_ref, load_sem.at[1]),
        pltpu.make_async_copy(grad_in, grad_ref, load_sem.at[2]),
        pltpu.make_async_copy(taps_in, taps_ref, load_sem.at[3]),
        pltpu.make_async_copy(gain_in, gain_ref, load_sem.at[4]),
    ]
    for k in (3, 0, 1, 2, 4):
        loads[k].start()
    pl.semaphore_wait(barrier, len(partners))

    def to_next(src, ext, send, recv, t):
        return pltpu.make_async_remote_copy(
            src_ref=src,
            dst_ref=ext.at[tile_at(t)],
            send_sem=send.at[0, t],
            recv_sem=recv.at[0, t],
            device_id=next_dev,
            device_id_type=MESH,
        )

    def to_prev(src, ext, send, recv, t):
        return pltpu.make_async_remote_copy(
            src_ref=src,
            dst_ref=ext.at[tile_at(8 + t)],
            send_sem=send.at[1, t],
            recv_sem=recv.at[1, t],
            device_id=prev_dev,
            device_id_type=MESH,
        )

    v_next = [to_next(value_in.at[tile_at(t)], vext, vsend, vrecv, t) for t in range(4)]
    v_prev = [to_prev(value_in.at[tile_at(t)], vext, vsend, vrecv, t) for t in range(4)]
    m_next = [to_next(mext.at[tile_at(4 + t)], mext, msend, mrecv, t) for t in range(4)]
    m_prev = [to_prev(mext.at[tile_at(4 + t)], mext, msend, mrecv, t) for t in range(4)]

    @pl.when(has_next)
    def _():
        for t in (3, 2, 1, 0):
            v_next[t].start()

    @pl.when(has_prev)
    def _():
        for t in range(4):
            v_prev[t].start()

    @pl.when(jnp.logical_not(has_prev))
    def _():
        vext[0:ROWS, :] = jnp.zeros((ROWS, WIDTH), BF16)
        mext[0:ROWS, :] = jnp.zeros((ROWS, WIDTH), BF16)

    @pl.when(jnp.logical_not(has_next))
    def _():
        vext[2 * ROWS : 3 * ROWS, :] = jnp.zeros((ROWS, WIDTH), BF16)
        mext[2 * ROWS : 3 * ROWS, :] = jnp.zeros((ROWS, WIDTH), BF16)

    loads[3].wait()
    taps = jnp.concatenate([taps_ref[...].astype(F32), jnp.zeros((4, 2048), F32)], axis=0)
    stacked = jnp.concatenate([taps[:, 128 * b : 128 * b + 128] for b in range(16)], axis=0)
    flip = (
        lax.broadcasted_iota(jnp.int32, (128, 128), 0)
        + lax.broadcasted_iota(jnp.int32, (128, 128), 1)
        == 127
    ).astype(BF16)
    turned = jnp.dot(stacked.astype(BF16), flip, preferred_element_type=F32)
    back = jnp.concatenate([turned[8 * b : 8 * b + 8] for b in reversed(range(16))], axis=1)
    for h in range(HEADS):
        build_band(back[h : h + 1], 1, ahead, h)
    loads[0].wait()
    for t in (4, 5, 6):
        make_pair(vext, vpairs, t)
    add_slots(ahead, vpairs, total, [4], fresh=True)
    for h in range(HEADS):
        build_band(taps[h : h + 1], 0, behind, h)

    def arrive(nexts, prevs, below, above):
        @pl.when(has_prev)
        def _():
            for t in below:
                nexts[t].wait_recv()

        @pl.when(has_next)
        def _():
            for t in above:
                prevs[t].wait_recv()

    def put_mixed(p, hp, block):
        mixed[tile_at(p), 128 * hp : 128 * hp + 128] = block

    for c in (1, 2, 3):
        arrive(v_next, v_prev, [4 - c], [c - 1])
        make_pair(vext, vpairs, 4 - c)
        make_pair(vext, vpairs, 6 + c)
        add_slots(ahead, vpairs, total, [4 - c, 4 + c])

    def between(h, carry):
        extra[h] = jnp.dot(ahead[h, 0], vpairs[h, 1], preferred_element_type=F32) + jnp.dot(
            ahead[h, 8], vpairs[h, 9], preferred_element_type=F32
        )
        return carry

    lax.fori_loop(0, HEADS, between, 0)
    inner_rows(total, extra, put_mixed)
    for k in (1, 2, 4):
        loads[k].wait()

    gain = gain_ref[...]

    def block_at(b):
        return pl.ds(pl.multiple_of(b * 128, 128), 128)

    def sums(stage, b, at):
        rows = block_at(b)
        hidden = gate_ref[rows, :].astype(F32) * mixed[rows, :]
        square = hidden * hidden
        inner = gain * grad_ref[rows, :].astype(F32) * hidden
        for k, v in ((0, square), (4, inner)):
            half = (v[:, :128] + v[:, 128:]).T
            chan_buf[stage, ch, pl.ds(k + at, 1), :] = jnp.sum(half, axis=0, keepdims=True)

    def inner_sums(i, carry):
        sums(0, i + 2, i)
        return carry

    def outer_sums(i, carry):
        sums(1, i + 4 * lax.div(i, 2), i)
        return carry

    def exchange(src_of, dst, send, recv, dev_of, order):
        return [
            pltpu.make_async_remote_copy(
                src_ref=src_of(j),
                dst_ref=dst,
                send_sem=send.at[j],
                recv_sem=recv.at[j],
                device_id=dev_of(j),
                device_id_type=MESH,
            )
            for j in order
        ]

    chan_copies = [
        exchange(
            lambda j, k=k: chan_buf.at[k, ch],
            chan_buf.at[k, ch],
            chan_send.at[k],
            chan_recv.at[k],
            chan_dev,
            far_first(chans),
        )
        for k in range(2)
    ]

    def scales(stage):
        for copy in chan_copies[stage]:
            copy.wait_recv()
        sums_all = chan_buf[stage, 0]
        for j in range(1, chans):
            sums_all = sums_all + chan_buf[stage, j]
        scale = lax.rsqrt(sums_all[0:4] / depth + EPS)
        row_scale[stage, 0:4, :] = scale
        row_scale[stage, 4:8, :] = scale * scale * sums_all[4:8] / depth

    gain_sum[...] = jnp.zeros((8, WIDTH), F32)

    def apply(stage, b, at):
        rows = block_at(b)

        def column(k):
            tall = jnp.broadcast_to(row_scale[stage, pl.ds(k + at, 1), :], (128, 128)).T
            return jnp.concatenate([tall, tall], axis=1)

        scale = column(0)
        pull = column(4)
        gate = gate_ref[rows, :].astype(F32)
        grad = grad_ref[rows, :].astype(F32)
        mix = mixed[rows, :]
        hidden = gate * mix
        scaled = hidden * scale
        normed_out[rows, :] = (scaled * gain).astype(BF16)
        hidden_grad = scale * (gain * grad - hidden * pull)
        gate_grad_out[rows, :] = (hidden_grad * mix).astype(BF16)
        mext[pl.ds(pl.multiple_of(ROWS + b * 128, 128), 128), :] = (hidden_grad * gate).astype(BF16)
        term = grad * scaled
        gain_sum[...] += jnp.sum(term.reshape(16, 8, WIDTH), axis=0)

    def apply_tile(t):
        def one(i, carry):
            if t in (1, 2):
                apply(0, 2 * t + i, 2 * t - 2 + i)
            else:
                apply(1, 2 * t + i, (0 if t == 0 else 2) + i)
            return carry

        lax.fori_loop(0, 2, one, 0)

    def send_next(*tiles):
        @pl.when(has_next)
        def _():
            for t in tiles:
                m_next[t].start()

    def send_prev(*tiles):
        @pl.when(has_prev)
        def _():
            for t in tiles:
                m_prev[t].start()

    lax.fori_loop(0, 4, inner_sums, 0)
    for copy in chan_copies[0]:
        copy.start()
    arrive(v_next, v_prev, [0], [3])
    make_pair(vext, vpairs, 0)
    make_pair(vext, vpairs, 10)
    add_slots(ahead, vpairs, total, [0, 8])
    outer_rows(total, put_mixed)
    lax.fori_loop(0, 4, outer_sums, 0)
    for copy in chan_copies[1]:
        copy.start()
    scales(0)
    apply_tile(1)
    send_prev(1)
    apply_tile(2)
    send_next(2, 1)
    send_prev(2)
    scales(1)
    apply_tile(0)
    apply_tile(3)

    for t in (4, 5, 6):
        make_pair(mext, mpairs, t)

    def lag_terms(h, carry):
        local = jnp.concatenate([mpairs[h, 4], mpairs[h, 6]], axis=1)
        for s in range(SLOTS):
            window = jnp.concatenate([vpairs[h, s], vpairs[h, s + 2]], axis=1)
            cross = lax.dot_general(
                window, local, (((1,), (1,)), ((), ())), preferred_element_type=F32
            )
            at = (17 - 2 * s) * 128
            right = cross[0:128, 128:256]
            lag_sum[:, at + 128 : at + 256] = right if s == 0 else right + held
            lag_sum[:, at : at + 128] = cross[0:128, 0:128] + cross[128:256, 128:256]
            held = cross[128:256, 0:128]
        lag_sum[:, 0:128] = held
        eight = lag_sum[0:8, :]
        for g in range(1, 16):
            eight = eight + pltpu.roll(lag_sum[8 * g : 8 * g + 8, :], SPAN - 8 * g, 1)
        sub = lax.broadcasted_iota(jnp.int32, (8, SPAN), 0)
        for bit in (1, 2, 4):
            eight = jnp.where((sub & bit) != 0, pltpu.roll(eight, SPAN - bit, 1), eight)
        line = jnp.sum(eight, axis=0, keepdims=True)
        for b in range(16):
            row = h * 16 + b
            cut_src[lax.div(row, cut), pl.ds(lax.rem(row, cut), 1), :] = line[
                :, 128 + 128 * b : 256 + 128 * b
            ]
        return carry

    lax.fori_loop(0, HEADS, lag_terms, 0)
    gains = jnp.sum(gain_sum[...], axis=0, keepdims=True)
    gain_rows = jnp.concatenate(
        [gains[:, :128], gains[:, 128:], jnp.zeros((6, 128), F32)], axis=0
    )
    for k in range(nz):
        cut_src[k, cut : cut + 8, :] = gain_rows

    cut_copies = exchange(
        lambda j: cut_src.at[z_of(j)], cut_buf.at[z], cut_send, cut_recv, z_dev, far_first(nz)
    )
    for copy in cut_copies:
        copy.start()
    send_next(3, 0)
    send_prev(0, 3)
    cut_buf[z] = cut_src[z]

    add_slots(behind, mpairs, total, [4], fresh=True)
    for copy in cut_copies:
        copy.wait_recv()
    part = cut_buf[0]
    for k in range(1, nz):
        part = part + cut_buf[k]
    all_buf[q] = part
    all_copies = exchange(
        lambda j: all_buf.at[q], all_buf.at[q], all_send, all_recv, q_dev, far_first_xy(nx, ny)
    )
    for copy in all_copies:
        copy.start()
    arrive(m_next, m_prev, [2, 1, 3], [1, 2, 0])
    for t in (1, 2, 3, 7, 8, 9):
        make_pair(mext, mpairs, t)
    add_slots(behind, mpairs, total, [1, 2, 3])
    add_slots(behind, mpairs, total, [5, 6, 7])
    for copy in all_copies:
        copy.wait_recv()
    part = all_buf[0]
    for k in range(1, nq):
        part = part + all_buf[k]
    gather_buf[z] = part[0:cut] * (1.0 / math.sqrt(ROWS * nseq * 64))
    gather_copies = exchange(
        lambda j: gather_buf.at[z], gather_buf.at[z], gather_send, gather_recv, z_dev, far_first(nz)
    )
    for copy in gather_copies:
        copy.start()
    gains = jnp.concatenate([part[cut : cut + 1], part[cut + 1 : cut + 2]], axis=1)
    gain_grad_ref[...] = gains * (1.0 / math.sqrt(ROWS * nseq))
    arrive(m_next, m_prev, [0], [3])
    make_pair(mext, mpairs, 0)
    make_pair(mext, mpairs, 10)
    add_slots(behind, mpairs, total, [0, 8])

    def put_grad(p, hp, block):
        value_grad_out[tile_at(p), 128 * hp : 128 * hp + 128] = block.astype(BF16)

    outer_rows(total, put_grad)
    inner_rows(total, None, put_grad)
    for copy in gather_copies:
        copy.wait_recv()
    for row in range(64):
        h, b = divmod(row, 16)
        k, r = divmod(row, cut)
        taps_grad_ref[h : h + 1, 128 * b : 128 * b + 128] = gather_buf[k, r : r + 1, :]

    for copy in chan_copies[0] + chan_copies[1] + cut_copies + all_copies + gather_copies:
        copy.wait_send()

    @pl.when(has_next)
    def _():
        for t in range(4):
            v_next[t].wait_send()
            m_next[t].wait_send()

    @pl.when(has_prev)
    def _():
        for t in range(4):
            v_prev[t].wait_send()
            m_prev[t].wait_send()


def write_out(*refs):
    sources, targets, sem = refs[:5], refs[5:10], refs[10]
    copies = [
        pltpu.make_async_copy(source, target, sem.at[k])
        for k, (source, target) in enumerate(zip(sources, targets))
    ]
    for copy in copies:
        copy.start()
    for copy in copies:
        copy.wait()


def on_device(dims, chans, gate_acts, value_acts, taps, norm_gain, out_grad):
    ny, nz, nx = dims
    nq = ny * nx
    cut = 64 // nz
    block = jax.ShapeDtypeStruct((ROWS, WIDTH), BF16)
    hbm = pl.BlockSpec(memory_space=pltpu.HBM)
    vmem = pl.BlockSpec(memory_space=pltpu.VMEM)
    dma = pltpu.SemaphoreType.DMA
    call = pl.pallas_call(
        functools.partial(kernel_body, dims, chans),
        out_shape=(
            block,
            block,
            block,
            jax.ShapeDtypeStruct((HEADS, 2048), F32),
            jax.ShapeDtypeStruct((1, WIDTH), F32),
        ),
        in_specs=[hbm] * 5,
        out_specs=(vmem,) * 5,
        scratch_shapes=[
            pltpu.VMEM((3 * ROWS, WIDTH), BF16),
            pltpu.VMEM((3 * ROWS, WIDTH), BF16),
            pltpu.VMEM((ROWS, WIDTH), BF16),
            pltpu.VMEM((ROWS, WIDTH), BF16),
            pltpu.VMEM((HEADS, 2048), BF16),
            pltpu.VMEM((1, WIDTH), F32),
            pltpu.VMEM((HEADS, SLOTS, TILE, TILE), BF16),
            pltpu.VMEM((HEADS, SLOTS, TILE, TILE), BF16),
            pltpu.VMEM((HEADS, 11, TILE, 128), BF16),
            pltpu.VMEM((HEADS, 11, TILE, 128), BF16),
            pltpu.VMEM((HEADS, TILE, TILE), F32),
            pltpu.VMEM((HEADS, TILE, 128), F32),
            pltpu.VMEM((ROWS, WIDTH), F32),
            pltpu.VMEM((128, SPAN), F32),
            pltpu.VMEM((2, chans, 8, 128), F32),
            pltpu.VMEM((2, 8, 128), F32),
            pltpu.VMEM((8, WIDTH), F32),
            pltpu.VMEM((nz, cut + 8, 128), F32),
            pltpu.VMEM((nz, cut + 8, 128), F32),
            pltpu.VMEM((nq, cut + 8, 128), F32),
            pltpu.VMEM((nz, cut, 128), F32),
            dma((5,)),
            dma((2, 4)),
            dma((2, 4)),
            dma((2, 4)),
            dma((2, 4)),
            dma((2, chans)),
            dma((2, chans)),
            dma((nz,)),
            dma((nz,)),
            dma((nq,)),
            dma((nq,)),
            dma((nz,)),
            dma((nz,)),
        ],
        compiler_params=pltpu.CompilerParams(
            collective_id=0, has_side_effects=True, vmem_limit_bytes=52 * 1024 * 1024
        ),
        cost_estimate=pl.CostEstimate(
            flops=3_700_000_000, bytes_accessed=6_000_000, transcendentals=1024
        ),
        name="toeplitz_mix",
    )
    operands = (gate_acts, value_acts, taps, norm_gain.reshape(1, WIDTH), out_grad)
    results = call(*[pltpu.with_memory_space_constraint(v, pltpu.HBM) for v in operands])
    normed, gate_grad, value_grad, taps_grad, gain_grad = pl.pallas_call(
        write_out,
        out_shape=[jax.ShapeDtypeStruct(r.shape, r.dtype) for r in results],
        in_specs=[vmem] * 5,
        out_specs=[hbm] * 5,
        scratch_shapes=[dma((5,))],
        compiler_params=pltpu.CompilerParams(vmem_limit_bytes=8 * 1024 * 1024),
        name="write_out",
    )(*results)
    return normed, gate_grad, value_grad, taps_grad, gain_grad.reshape(WIDTH)


def solution(mesh, dims=(2, 8, 4)):
    placed = (P("seq", "chan"), P("seq", "chan"), P("chan", None), P("chan"), P("seq", "chan"))
    return jax.shard_map(
        functools.partial(on_device, dims, mesh.shape["chan"]),
        mesh=mesh,
        in_specs=placed,
        out_specs=(
            P("seq", "chan"),
            P("seq", "chan"),
            P("seq", "chan"),
            P("chan", None),
            P("chan"),
        ),
        check_vma=False,
    )
```

```python
import functools
import math

import jax
import jax.numpy as jnp
from jax import lax
from jax.experimental import pallas as pl
from jax.experimental.pallas import tpu as pltpu
from jax.sharding import PartitionSpec as P

EPS = 1e-06
ROWS = 1024
WIDTH = 256
TILE = 256
HEADS = 4
SLOTS = 9
SPAN = 2432
F32 = jnp.float32
BF16 = jnp.bfloat16
MESH = pl.DeviceIdType.MESH


def far_first(count):
    return sorted(range(1, count), key=lambda j: -min(j, count - j))


def far_first_xy(nx, ny):
    return sorted(range(1, nx * ny), key=lambda j: -min(j % nx, nx - j % nx))


def tile_at(t):
    return pl.ds(t * TILE, TILE)


def build_band(row, first, band, h):
    wide = jnp.concatenate(
        [jnp.broadcast_to(row, (8, 2048)), jnp.zeros((8, SPAN - 2048), F32)], axis=1
    )
    sub = lax.broadcasted_iota(jnp.int32, (8, SPAN), 0)
    if first:
        wide = pltpu.roll(wide, first, 1)
    for bit in (1, 2, 4):
        wide = jnp.where((sub & bit) != 0, pltpu.roll(wide, bit, 1), wide)
    base = jnp.concatenate([wide, pltpu.roll(wide, 8, 1)], axis=0)
    for g in range(8):
        part = (pltpu.roll(base, 16 * g, 1) if g else base).astype(BF16)
        low = jnp.concatenate([jnp.zeros((16, 128), BF16), part[:, : SPAN - 256]], axis=1)
        for s in range(SLOTS):
            band[h, s, 16 * g : 16 * g + 16, :] = part[:, 256 * s : 256 * s + 256]
            band[h, s, 128 + 16 * g : 144 + 16 * g, :] = low[:, 256 * s : 256 * s + 256]


def swap_halves(x):
    return jnp.concatenate([x[:, 64:], x[:, :64]], axis=1)


def make_pair(ext, pairs, t):
    low = lax.broadcasted_iota(jnp.int32, (TILE, 128), 1) < 64
    for hp in range(2):
        a = ext[tile_at(t), 128 * hp : 128 * hp + 128]
        b = ext[tile_at(t + 1), 128 * hp : 128 * hp + 128]
        crossed = swap_halves(jnp.where(low, b, a))
        pairs[2 * hp, t] = jnp.where(low, a, crossed)
        pairs[2 * hp + 1, t] = jnp.where(low, crossed, b)


def add_slots(band, pairs, total, slots, fresh=False):
    def one(h, carry):
        acc = None
        for s in slots:
            right = jnp.concatenate([pairs[h, s], pairs[h, s + 2]], axis=1)
            term = jnp.dot(band[h, s], right, preferred_element_type=F32)
            acc = term if acc is None else acc + term
        total[h] = acc if fresh else total[h] + acc
        return carry

    lax.fori_loop(0, HEADS, one, 0)


def outer_rows(total, put):
    low = lax.broadcasted_iota(jnp.int32, (TILE, 128), 1) < 64
    for hp in range(2):
        a = total[2 * hp, :, 0:128]
        b = total[2 * hp + 1, :, 0:128]
        put(0, hp, jnp.where(low, a, swap_halves(b)))
        a = total[2 * hp, :, 128:256]
        b = total[2 * hp + 1, :, 128:256]
        put(3, hp, jnp.where(low, swap_halves(a), b))


def all_rows(total, put):
    low = lax.broadcasted_iota(jnp.int32, (TILE, 128), 1) < 64
    for hp in range(2):
        for pp in range(2):
            a = total[2 * hp, :, 128 * pp : 128 * pp + 128]
            b = total[2 * hp + 1, :, 128 * pp : 128 * pp + 128]
            crossed = swap_halves(jnp.where(low, b, a))
            put(2 * pp, hp, jnp.where(low, a, crossed))
            put(2 * pp + 1, hp, jnp.where(low, crossed, b))


def inner_rows(total, extra, put):
    low = lax.broadcasted_iota(jnp.int32, (TILE, 128), 1) < 64
    for hp in range(2):
        more_a = extra[2 * hp]
        more_b = extra[2 * hp + 1]
        more = swap_halves(jnp.where(low, more_b, more_a))
        a = total[2 * hp, :, 0:128]
        b = total[2 * hp + 1, :, 0:128]
        put(1, hp, jnp.where(low, swap_halves(a) + more_a, b + more))
        a = total[2 * hp, :, 128:256]
        b = total[2 * hp + 1, :, 128:256]
        put(2, hp, jnp.where(low, a + more, swap_halves(b) + more_b))


def kernel_body(
    dims,
    chans,
    gate_in,
    value_in,
    taps_in,
    gain_in,
    grad_in,
    normed_out,
    gate_grad_out,
    value_grad_out,
    taps_grad_ref,
    gain_grad_ref,
    vext,
    mext,
    gate_ref,
    grad_ref,
    taps_ref,
    gain_ref,
    ahead,
    behind,
    vpairs,
    mpairs,
    total,
    extra,
    mixed,
    lag_sum,
    chan_buf,
    row_scale,
    gain_sum,
    cut_src,
    cut_buf,
    all_buf,
    gather_buf,
    load_sem,
    vsend,
    vrecv,
    msend,
    mrecv,
    chan_send,
    chan_recv,
    cut_send,
    cut_recv,
    all_send,
    all_recv,
    gather_send,
    gather_recv,
):
    ny, nz, nx = dims
    nseq = ny * nz * nx
    nq = ny * nx
    cut = 64 // nz
    depth = WIDTH * chans
    me = lax.axis_index("seq")
    ch = lax.axis_index("chan")
    x = lax.rem(me, nx)
    z = lax.rem(lax.div(me, nx), nz)
    y = lax.div(me, nx * nz)
    q = y * nx + x
    has_prev = me > 0
    has_next = me < nseq - 1
    prev_dev = (lax.rem(me + nseq - 1, nseq), ch)
    next_dev = (lax.rem(me + 1, nseq), ch)

    def chan_dev(j):
        return (me, lax.rem(ch + j, chans))

    def z_of(j):
        return lax.rem(z + j, nz)

    def z_dev(j):
        return ((y * nz + z_of(j)) * nx + x, ch)

    def q_dev(j):
        other = lax.rem(q + j, nq)
        return ((lax.div(other, nx) * nz + z) * nx + lax.rem(other, nx), ch)

    barrier = pltpu.get_barrier_semaphore()
    partners = (
        [prev_dev, next_dev]
        + [z_dev(j) for j in far_first(nz)]
        + [chan_dev(j) for j in far_first(chans)]
        + [q_dev(j) for j in far_first_xy(nx, ny)]
    )
    for dev in partners:
        pl.semaphore_signal(barrier, inc=1, device_id=dev, device_id_type=MESH)

    loads = [
        pltpu.make_async_copy(value_in, vext.at[pl.ds(ROWS, ROWS)], load_sem.at[0]),
        pltpu.make_async_copy(gate_in, gate_ref, load_sem.at[1]),
        pltpu.make_async_copy(grad_in, grad_ref, load_sem.at[2]),
        pltpu.make_async_copy(taps_in, taps_ref, load_sem.at[3]),
        pltpu.make_async_copy(gain_in, gain_ref, load_sem.at[4]),
    ]
    for k in (3, 0, 1, 2, 4):
        loads[k].start()
    pl.semaphore_wait(barrier, len(partners))

    def to_next(src, ext, send, recv, t):
        return pltpu.make_async_remote_copy(
            src_ref=src,
            dst_ref=ext.at[tile_at(t)],
            send_sem=send.at[0, t],
            recv_sem=recv.at[0, t],
            device_id=next_dev,
            device_id_type=MESH,
        )

    def to_prev(src, ext, send, recv, t):
        return pltpu.make_async_remote_copy(
            src_ref=src,
            dst_ref=ext.at[tile_at(8 + t)],
            send_sem=send.at[1, t],
            recv_sem=recv.at[1, t],
            device_id=prev_dev,
            device_id_type=MESH,
        )

    v_next = [to_next(value_in.at[tile_at(t)], vext, vsend, vrecv, t) for t in range(4)]
    v_prev = [to_prev(value_in.at[tile_at(t)], vext, vsend, vrecv, t) for t in range(4)]
    m_next = [to_next(mext.at[tile_at(4 + t)], mext, msend, mrecv, t) for t in range(4)]
    m_prev = [to_prev(mext.at[tile_at(4 + t)], mext, msend, mrecv, t) for t in range(4)]

    @pl.when(has_next)
    def _():
        for t in (3, 2, 1, 0):
            v_next[t].start()

    @pl.when(has_prev)
    def _():
        for t in range(4):
            v_prev[t].start()

    @pl.when(jnp.logical_not(has_prev))
    def _():
        vext[0:ROWS, :] = jnp.zeros((ROWS, WIDTH), BF16)
        mext[0:ROWS, :] = jnp.zeros((ROWS, WIDTH), BF16)

    @pl.when(jnp.logical_not(has_next))
    def _():
        vext[2 * ROWS : 3 * ROWS, :] = jnp.zeros((ROWS, WIDTH), BF16)
        mext[2 * ROWS : 3 * ROWS, :] = jnp.zeros((ROWS, WIDTH), BF16)

    loads[3].wait()
    taps = jnp.concatenate([taps_ref[...].astype(F32), jnp.zeros((4, 2048), F32)], axis=0)
    stacked = jnp.concatenate([taps[:, 128 * b : 128 * b + 128] for b in range(16)], axis=0)
    flip = (
        lax.broadcasted_iota(jnp.int32, (128, 128), 0)
        + lax.broadcasted_iota(jnp.int32, (128, 128), 1)
        == 127
    ).astype(BF16)
    turned = jnp.dot(stacked.astype(BF16), flip, preferred_element_type=F32)
    back = jnp.concatenate([turned[8 * b : 8 * b + 8] for b in reversed(range(16))], axis=1)
    for h in range(HEADS):
        build_band(back[h : h + 1], 1, ahead, h)
    loads[0].wait()
    for t in (4, 5, 6):
        make_pair(vext, vpairs, t)
    add_slots(ahead, vpairs, total, [4], fresh=True)
    for h in range(HEADS):
        build_band(taps[h : h + 1], 0, behind, h)

    def arrive(nexts, prevs, below, above):
        @pl.when(has_prev)
        def _():
            for t in below:
                nexts[t].wait_recv()

        @pl.when(has_next)
        def _():
            for t in above:
                prevs[t].wait_recv()

    def put_mixed(p, hp, block):
        mixed[tile_at(p), 128 * hp : 128 * hp + 128] = block

    for c in (1, 2, 3):
        arrive(v_next, v_prev, [4 - c], [c - 1])
        make_pair(vext, vpairs, 4 - c)
        make_pair(vext, vpairs, 6 + c)
        add_slots(ahead, vpairs, total, [4 - c, 4 + c])

    def between(h, carry):
        extra[h] = jnp.dot(ahead[h, 0], vpairs[h, 1], preferred_element_type=F32) + jnp.dot(
            ahead[h, 8], vpairs[h, 9], preferred_element_type=F32
        )
        return carry

    lax.fori_loop(0, HEADS, between, 0)
    inner_rows(total, extra, put_mixed)
    for k in (1, 2, 4):
        loads[k].wait()

    gain = gain_ref[...]

    def block_at(b):
        return pl.ds(pl.multiple_of(b * 128, 128), 128)

    def sums(stage, b, at):
        rows = block_at(b)
        hidden = gate_ref[rows, :].astype(F32) * mixed[rows, :]
        square = hidden * hidden
        inner = gain * grad_ref[rows, :].astype(F32) * hidden
        for k, v in ((0, square), (4, inner)):
            half = (v[:, :128] + v[:, 128:]).T
            chan_buf[stage, ch, pl.ds(k + at, 1), :] = jnp.sum(half, axis=0, keepdims=True)

    def inner_sums(i, carry):
        sums(0, i + 2, i)
        return carry

    def outer_sums(i, carry):
        sums(1, i + 4 * lax.div(i, 2), i)
        return carry

    def exchange(src_of, dst, send, recv, dev_of, order):
        return [
            pltpu.make_async_remote_copy(
                src_ref=src_of(j),
                dst_ref=dst,
                send_sem=send.at[j],
                recv_sem=recv.at[j],
                device_id=dev_of(j),
                device_id_type=MESH,
            )
            for j in order
        ]

    chan_copies = [
        exchange(
            lambda j, k=k: chan_buf.at[k, ch],
            chan_buf.at[k, ch],
            chan_send.at[k],
            chan_recv.at[k],
            chan_dev,
            far_first(chans),
        )
        for k in range(2)
    ]

    def scales(stage):
        for copy in chan_copies[stage]:
            copy.wait_recv()
        sums_all = chan_buf[stage, 0]
        for j in range(1, chans):
            sums_all = sums_all + chan_buf[stage, j]
        scale = lax.rsqrt(sums_all[0:4] / depth + EPS)
        row_scale[stage, 0:4, :] = scale
        row_scale[stage, 4:8, :] = scale * scale * sums_all[4:8] / depth

    gain_sum[...] = jnp.zeros((8, WIDTH), F32)

    def apply(stage, b, at):
        rows = block_at(b)

        def column(k):
            tall = jnp.broadcast_to(row_scale[stage, pl.ds(k + at, 1), :], (128, 128)).T
            return jnp.concatenate([tall, tall], axis=1)

        scale = column(0)
        pull = column(4)
        gate = gate_ref[rows, :].astype(F32)
        grad = grad_ref[rows, :].astype(F32)
        mix = mixed[rows, :]
        hidden = gate * mix
        scaled = hidden * scale
        normed_out[rows, :] = (scaled * gain).astype(BF16)
        hidden_grad = scale * (gain * grad - hidden * pull)
        gate_grad_out[rows, :] = (hidden_grad * mix).astype(BF16)
        mext[pl.ds(pl.multiple_of(ROWS + b * 128, 128), 128), :] = (hidden_grad * gate).astype(BF16)
        term = grad * scaled
        gain_sum[...] += jnp.sum(term.reshape(16, 8, WIDTH), axis=0)

    def apply_tile(t):
        def one(i, carry):
            if t in (1, 2):
                apply(0, 2 * t + i, 2 * t - 2 + i)
            else:
                apply(1, 2 * t + i, (0 if t == 0 else 2) + i)
            return carry

        lax.fori_loop(0, 2, one, 0)

    def send_next(*tiles):
        @pl.when(has_next)
        def _():
            for t in tiles:
                m_next[t].start()

    def send_prev(*tiles):
        @pl.when(has_prev)
        def _():
            for t in tiles:
                m_prev[t].start()

    lax.fori_loop(0, 4, inner_sums, 0)
    for copy in chan_copies[0]:
        copy.start()
    arrive(v_next, v_prev, [0], [3])
    make_pair(vext, vpairs, 0)
    make_pair(vext, vpairs, 10)
    add_slots(ahead, vpairs, total, [0, 8])
    outer_rows(total, put_mixed)
    lax.fori_loop(0, 4, outer_sums, 0)
    for copy in chan_copies[1]:
        copy.start()
    scales(0)
    apply_tile(1)
    send_prev(1)
    apply_tile(2)
    send_next(2, 1)
    send_prev(2)
    scales(1)
    apply_tile(0)
    apply_tile(3)

    for t in (4, 6):
        make_pair(mext, mpairs, t)

    def lag_terms(h, carry):
        local = jnp.concatenate([mpairs[h, 4], mpairs[h, 6]], axis=1)
        for s in range(SLOTS):
            window = jnp.concatenate([vpairs[h, s], vpairs[h, s + 2]], axis=1)
            cross = lax.dot_general(
                window, local, (((1,), (1,)), ((), ())), preferred_element_type=F32
            )
            at = (17 - 2 * s) * 128
            right = cross[0:128, 128:256]
            lag_sum[:, at + 128 : at + 256] = right if s == 0 else right + held
            lag_sum[:, at : at + 128] = cross[0:128, 0:128] + cross[128:256, 128:256]
            held = cross[128:256, 0:128]
        lag_sum[:, 0:128] = held
        eight = lag_sum[0:8, :]
        for g in range(1, 16):
            eight = eight + pltpu.roll(lag_sum[8 * g : 8 * g + 8, :], SPAN - 8 * g, 1)
        sub = lax.broadcasted_iota(jnp.int32, (8, SPAN), 0)
        for bit in (1, 2, 4):
            eight = jnp.where((sub & bit) != 0, pltpu.roll(eight, SPAN - bit, 1), eight)
        line = jnp.sum(eight, axis=0, keepdims=True)
        for b in range(16):
            row = h * 16 + b
            cut_src[lax.div(row, cut), pl.ds(lax.rem(row, cut), 1), :] = line[
                :, 128 + 128 * b : 256 + 128 * b
            ]
        return carry

    lax.fori_loop(0, HEADS, lag_terms, 0)
    gains = jnp.sum(gain_sum[...], axis=0, keepdims=True)
    gain_rows = jnp.concatenate([gains[:, :128], gains[:, 128:]], axis=0)
    for k in range(nz):
        cut_src[k, cut : cut + 2, :] = gain_rows

    cut_copies = exchange(
        lambda j: cut_src.at[z_of(j)], cut_buf.at[z], cut_send, cut_recv, z_dev, far_first(nz)
    )
    for copy in cut_copies:
        copy.start()
    send_next(3, 0)
    send_prev(0, 3)
    cut_buf[z] = cut_src[z]

    add_slots(behind, mpairs, total, [4], fresh=True)
    for copy in cut_copies:
        copy.wait_recv()
    part = cut_buf[0]
    for k in range(1, nz):
        part = part + cut_buf[k]
    all_buf[q] = part
    all_copies = exchange(
        lambda j: all_buf.at[q], all_buf.at[q], all_send, all_recv, q_dev, far_first_xy(nx, ny)
    )
    for copy in all_copies:
        copy.start()
    arrive(m_next, m_prev, [2, 1, 3], [1, 2, 0])
    for t in (1, 2, 3, 5, 7, 8, 9):
        make_pair(mext, mpairs, t)
    add_slots(behind, mpairs, total, [1, 2, 3])
    add_slots(behind, mpairs, total, [5, 6, 7])
    for copy in all_copies:
        copy.wait_recv()
    part = all_buf[0]
    for k in range(1, nq):
        part = part + all_buf[k]
    gather_buf[z] = part[0:cut] * (1.0 / math.sqrt(ROWS * nseq * 64))
    gather_copies = exchange(
        lambda j: gather_buf.at[z], gather_buf.at[z], gather_send, gather_recv, z_dev, far_first(nz)
    )
    for copy in gather_copies:
        copy.start()
    gains = jnp.concatenate([part[cut : cut + 1], part[cut + 1 : cut + 2]], axis=1)
    gain_grad_ref[...] = gains * (1.0 / math.sqrt(ROWS * nseq))
    arrive(m_next, m_prev, [0], [3])
    make_pair(mext, mpairs, 0)
    make_pair(mext, mpairs, 10)
    add_slots(behind, mpairs, total, [0, 8])

    def put_grad(p, hp, block):
        value_grad_out[tile_at(p), 128 * hp : 128 * hp + 128] = block.astype(BF16)

    all_rows(total, put_grad)
    for copy in gather_copies:
        copy.wait_recv()
    for row in range(64):
        h, b = divmod(row, 16)
        k, r = divmod(row, cut)
        taps_grad_ref[h : h + 1, 128 * b : 128 * b + 128] = gather_buf[k, r : r + 1, :]

    for copy in chan_copies[0] + chan_copies[1] + cut_copies + all_copies + gather_copies:
        copy.wait_send()

    @pl.when(has_next)
    def _():
        for t in range(4):
            v_next[t].wait_send()
            m_next[t].wait_send()

    @pl.when(has_prev)
    def _():
        for t in range(4):
            v_prev[t].wait_send()
            m_prev[t].wait_send()


def write_out(*refs):
    sources, targets, sem = refs[:5], refs[5:10], refs[10]
    copies = [
        pltpu.make_async_copy(source, target, sem.at[k])
        for k, (source, target) in enumerate(zip(sources, targets))
    ]
    for copy in copies:
        copy.start()
    for copy in copies:
        copy.wait()


def on_device(dims, chans, gate_acts, value_acts, taps, norm_gain, out_grad):
    ny, nz, nx = dims
    nq = ny * nx
    cut = 64 // nz
    block = jax.ShapeDtypeStruct((ROWS, WIDTH), BF16)
    hbm = pl.BlockSpec(memory_space=pltpu.HBM)
    vmem = pl.BlockSpec(memory_space=pltpu.VMEM)
    dma = pltpu.SemaphoreType.DMA
    call = pl.pallas_call(
        functools.partial(kernel_body, dims, chans),
        out_shape=(
            block,
            block,
            block,
            jax.ShapeDtypeStruct((HEADS, 2048), F32),
            jax.ShapeDtypeStruct((1, WIDTH), F32),
        ),
        in_specs=[hbm] * 5,
        out_specs=(vmem,) * 5,
        scratch_shapes=[
            pltpu.VMEM((3 * ROWS, WIDTH), BF16),
            pltpu.VMEM((3 * ROWS, WIDTH), BF16),
            pltpu.VMEM((ROWS, WIDTH), BF16),
            pltpu.VMEM((ROWS, WIDTH), BF16),
            pltpu.VMEM((HEADS, 2048), BF16),
            pltpu.VMEM((1, WIDTH), F32),
            pltpu.VMEM((HEADS, SLOTS, TILE, TILE), BF16),
            pltpu.VMEM((HEADS, SLOTS, TILE, TILE), BF16),
            pltpu.VMEM((HEADS, 11, TILE, 128), BF16),
            pltpu.VMEM((HEADS, 11, TILE, 128), BF16),
            pltpu.VMEM((HEADS, TILE, TILE), F32),
            pltpu.VMEM((HEADS, TILE, 128), F32),
            pltpu.VMEM((ROWS, WIDTH), F32),
            pltpu.VMEM((128, SPAN), F32),
            pltpu.VMEM((2, chans, 8, 128), F32),
            pltpu.VMEM((2, 8, 128), F32),
            pltpu.VMEM((8, WIDTH), F32),
            pltpu.VMEM((nz, cut + 2, 128), F32),
            pltpu.VMEM((nz, cut + 2, 128), F32),
            pltpu.VMEM((nq, cut + 2, 128), F32),
            pltpu.VMEM((nz, cut, 128), F32),
            dma((5,)),
            dma((2, 4)),
            dma((2, 4)),
            dma((2, 4)),
            dma((2, 4)),
            dma((2, chans)),
            dma((2, chans)),
            dma((nz,)),
            dma((nz,)),
            dma((nq,)),
            dma((nq,)),
            dma((nz,)),
            dma((nz,)),
        ],
        compiler_params=pltpu.CompilerParams(
            collective_id=0, has_side_effects=True, vmem_limit_bytes=52 * 1024 * 1024
        ),
        cost_estimate=pl.CostEstimate(
            flops=3_700_000_000, bytes_accessed=6_000_000, transcendentals=1024
        ),
        name="toeplitz_mix",
    )
    operands = (gate_acts, value_acts, taps, norm_gain.reshape(1, WIDTH), out_grad)
    results = call(*[pltpu.with_memory_space_constraint(v, pltpu.HBM) for v in operands])
    normed, gate_grad, value_grad, taps_grad, gain_grad = pl.pallas_call(
        write_out,
        out_shape=[jax.ShapeDtypeStruct(r.shape, r.dtype) for r in results],
        in_specs=[vmem] * 5,
        out_specs=[hbm] * 5,
        scratch_shapes=[dma((5,))],
        compiler_params=pltpu.CompilerParams(vmem_limit_bytes=8 * 1024 * 1024),
        name="write_out",
    )(*results)
    return normed, gate_grad, value_grad, taps_grad, gain_grad.reshape(WIDTH)


def solution(mesh, dims=(2, 8, 4)):
    placed = (P("seq", "chan"), P("seq", "chan"), P("chan", None), P("chan"), P("seq", "chan"))
    return jax.shard_map(
        functools.partial(on_device, dims, mesh.shape["chan"]),
        mesh=mesh,
        in_specs=placed,
        out_specs=(
            P("seq", "chan"),
            P("seq", "chan"),
            P("seq", "chan"),
            P("chan", None),
            P("chan"),
        ),
        check_vma=False,
    )
```

```python
import functools
import math

import jax
import jax.numpy as jnp
from jax import lax
from jax.experimental import pallas as pl
from jax.experimental.pallas import tpu as pltpu
from jax.sharding import PartitionSpec as P

EPS = 1e-06
ROWS = 1024
WIDTH = 256
TILE = 256
HEADS = 4
SLOTS = 9
SPAN = 2432
F32 = jnp.float32
BF16 = jnp.bfloat16
MESH = pl.DeviceIdType.MESH


def far_first(count):
    return sorted(range(1, count), key=lambda j: -min(j, count - j))


def far_first_xy(nx, ny):
    return sorted(range(1, nx * ny), key=lambda j: -min(j % nx, nx - j % nx))


def tile_at(t):
    return pl.ds(t * TILE, TILE)


def build_band(row, first, band, h):
    wide = jnp.concatenate(
        [jnp.broadcast_to(row, (8, 2048)), jnp.zeros((8, SPAN - 2048), F32)], axis=1
    )
    sub = lax.broadcasted_iota(jnp.int32, (8, SPAN), 0)
    if first:
        wide = pltpu.roll(wide, first, 1)
    for bit in (1, 2, 4):
        wide = jnp.where((sub & bit) != 0, pltpu.roll(wide, bit, 1), wide)
    base = jnp.concatenate([wide, pltpu.roll(wide, 8, 1)], axis=0)
    for g in range(8):
        part = (pltpu.roll(base, 16 * g, 1) if g else base).astype(BF16)
        low = jnp.concatenate([jnp.zeros((16, 128), BF16), part[:, : SPAN - 256]], axis=1)
        for s in range(SLOTS):
            band[h, s, 16 * g : 16 * g + 16, :] = part[:, 256 * s : 256 * s + 256]
            band[h, s, 128 + 16 * g : 144 + 16 * g, :] = low[:, 256 * s : 256 * s + 256]


def swap_halves(x):
    return jnp.concatenate([x[:, 64:], x[:, :64]], axis=1)


def make_pair(ext, pairs, t):
    low = lax.broadcasted_iota(jnp.int32, (TILE, 128), 1) < 64
    for hp in range(2):
        a = ext[tile_at(t), 128 * hp : 128 * hp + 128]
        b = ext[tile_at(t + 1), 128 * hp : 128 * hp + 128]
        crossed = swap_halves(jnp.where(low, b, a))
        pairs[2 * hp, t] = jnp.where(low, a, crossed)
        pairs[2 * hp + 1, t] = jnp.where(low, crossed, b)


def add_slots(band, pairs, total, slots, fresh=False):
    def one(h, carry):
        acc = None
        for s in slots:
            right = jnp.concatenate([pairs[h, s], pairs[h, s + 2]], axis=1)
            term = jnp.dot(band[h, s], right, preferred_element_type=F32)
            acc = term if acc is None else acc + term
        total[h] = acc if fresh else total[h] + acc
        return carry

    lax.fori_loop(0, HEADS, one, 0)


def outer_rows(total, put):
    low = lax.broadcasted_iota(jnp.int32, (TILE, 128), 1) < 64
    for hp in range(2):
        a = total[2 * hp, :, 0:128]
        b = total[2 * hp + 1, :, 0:128]
        put(0, hp, jnp.where(low, a, swap_halves(b)))
        a = total[2 * hp, :, 128:256]
        b = total[2 * hp + 1, :, 128:256]
        put(3, hp, jnp.where(low, swap_halves(a), b))


def all_rows(total, put):
    low = lax.broadcasted_iota(jnp.int32, (TILE, 128), 1) < 64
    for hp in range(2):
        for pp in range(2):
            a = total[2 * hp, :, 128 * pp : 128 * pp + 128]
            b = total[2 * hp + 1, :, 128 * pp : 128 * pp + 128]
            crossed = swap_halves(jnp.where(low, b, a))
            put(2 * pp, hp, jnp.where(low, a, crossed))
            put(2 * pp + 1, hp, jnp.where(low, crossed, b))


def inner_rows(total, extra, put):
    low = lax.broadcasted_iota(jnp.int32, (TILE, 128), 1) < 64
    for hp in range(2):
        more_a = extra[2 * hp]
        more_b = extra[2 * hp + 1]
        more = swap_halves(jnp.where(low, more_b, more_a))
        a = total[2 * hp, :, 0:128]
        b = total[2 * hp + 1, :, 0:128]
        put(1, hp, jnp.where(low, swap_halves(a) + more_a, b + more))
        a = total[2 * hp, :, 128:256]
        b = total[2 * hp + 1, :, 128:256]
        put(2, hp, jnp.where(low, a + more, swap_halves(b) + more_b))


def kernel_body(
    dims,
    chans,
    gate_in,
    value_in,
    taps_in,
    gain_in,
    grad_in,
    normed_out,
    gate_grad_out,
    value_grad_out,
    taps_grad_ref,
    gain_grad_ref,
    vext,
    mext,
    gate_ref,
    grad_ref,
    taps_ref,
    gain_ref,
    ahead,
    behind,
    vpairs,
    mpairs,
    total,
    extra,
    mixed,
    lag_sum,
    chan_buf,
    row_scale,
    gain_sum,
    cut_src,
    cut_buf,
    all_buf,
    gather_buf,
    load_sem,
    vsend,
    vrecv,
    msend,
    mrecv,
    chan_send,
    chan_recv,
    cut_send,
    cut_recv,
    all_send,
    all_recv,
    gather_send,
    gather_recv,
):
    ny, nz, nx = dims
    nseq = ny * nz * nx
    nq = ny * nx
    cut = 64 // nz
    depth = WIDTH * chans
    me = lax.axis_index("seq")
    ch = lax.axis_index("chan")
    x = lax.rem(me, nx)
    z = lax.rem(lax.div(me, nx), nz)
    y = lax.div(me, nx * nz)
    q = y * nx + x
    has_prev = me > 0
    has_next = me < nseq - 1
    prev_dev = (lax.rem(me + nseq - 1, nseq), ch)
    next_dev = (lax.rem(me + 1, nseq), ch)

    def chan_dev(j):
        return (me, lax.rem(ch + j, chans))

    def z_of(j):
        return lax.rem(z + j, nz)

    def z_dev(j):
        return ((y * nz + z_of(j)) * nx + x, ch)

    def q_dev(j):
        other = lax.rem(q + j, nq)
        return ((lax.div(other, nx) * nz + z) * nx + lax.rem(other, nx), ch)

    barrier = pltpu.get_barrier_semaphore()
    partners = (
        [prev_dev, next_dev]
        + [z_dev(j) for j in far_first(nz)]
        + [chan_dev(j) for j in far_first(chans)]
        + [q_dev(j) for j in far_first_xy(nx, ny)]
    )
    for dev in partners:
        pl.semaphore_signal(barrier, inc=1, device_id=dev, device_id_type=MESH)

    loads = [
        pltpu.make_async_copy(value_in, vext.at[pl.ds(ROWS, ROWS)], load_sem.at[0]),
        pltpu.make_async_copy(gate_in, gate_ref, load_sem.at[1]),
        pltpu.make_async_copy(grad_in, grad_ref, load_sem.at[2]),
        pltpu.make_async_copy(taps_in, taps_ref, load_sem.at[3]),
        pltpu.make_async_copy(gain_in, gain_ref, load_sem.at[4]),
    ]
    for k in (3, 0, 1, 2, 4):
        loads[k].start()
    pl.semaphore_wait(barrier, len(partners))

    def to_next(src, ext, send, recv, t):
        return pltpu.make_async_remote_copy(
            src_ref=src,
            dst_ref=ext.at[tile_at(t)],
            send_sem=send.at[0, t],
            recv_sem=recv.at[0, t],
            device_id=next_dev,
            device_id_type=MESH,
        )

    def to_prev(src, ext, send, recv, t):
        return pltpu.make_async_remote_copy(
            src_ref=src,
            dst_ref=ext.at[tile_at(8 + t)],
            send_sem=send.at[1, t],
            recv_sem=recv.at[1, t],
            device_id=prev_dev,
            device_id_type=MESH,
        )

    v_next = [to_next(value_in.at[tile_at(t)], vext, vsend, vrecv, t) for t in range(4)]
    v_prev = [to_prev(value_in.at[tile_at(t)], vext, vsend, vrecv, t) for t in range(4)]
    m_next = [to_next(mext.at[tile_at(4 + t)], mext, msend, mrecv, t) for t in range(4)]
    m_prev = [to_prev(mext.at[tile_at(4 + t)], mext, msend, mrecv, t) for t in range(4)]

    @pl.when(has_next)
    def _():
        for t in (3, 2, 1, 0):
            v_next[t].start()

    @pl.when(has_prev)
    def _():
        for t in range(4):
            v_prev[t].start()

    @pl.when(jnp.logical_not(has_prev))
    def _():
        vext[0:ROWS, :] = jnp.zeros((ROWS, WIDTH), BF16)
        mext[0:ROWS, :] = jnp.zeros((ROWS, WIDTH), BF16)

    @pl.when(jnp.logical_not(has_next))
    def _():
        vext[2 * ROWS : 3 * ROWS, :] = jnp.zeros((ROWS, WIDTH), BF16)
        mext[2 * ROWS : 3 * ROWS, :] = jnp.zeros((ROWS, WIDTH), BF16)

    loads[3].wait()
    taps = jnp.concatenate([taps_ref[...].astype(F32), jnp.zeros((4, 2048), F32)], axis=0)
    stacked = jnp.concatenate([taps[:, 128 * b : 128 * b + 128] for b in range(16)], axis=0)
    flip = (
        lax.broadcasted_iota(jnp.int32, (128, 128), 0)
        + lax.broadcasted_iota(jnp.int32, (128, 128), 1)
        == 127
    ).astype(BF16)
    turned = jnp.dot(stacked.astype(BF16), flip, preferred_element_type=F32)
    back = jnp.concatenate([turned[8 * b : 8 * b + 8] for b in reversed(range(16))], axis=1)
    for h in range(HEADS):
        build_band(back[h : h + 1], 1, ahead, h)
    loads[0].wait()
    for t in (4, 5, 6):
        make_pair(vext, vpairs, t)
    add_slots(ahead, vpairs, total, [4], fresh=True)
    for h in range(HEADS):
        build_band(taps[h : h + 1], 0, behind, h)

    def arrive(nexts, prevs, below, above):
        @pl.when(has_prev)
        def _():
            for t in below:
                nexts[t].wait_recv()

        @pl.when(has_next)
        def _():
            for t in above:
                prevs[t].wait_recv()

    def put_mixed(p, hp, block):
        mixed[tile_at(p), 128 * hp : 128 * hp + 128] = block

    for c in (1, 2, 3):
        arrive(v_next, v_prev, [4 - c], [c - 1])
        make_pair(vext, vpairs, 4 - c)
        make_pair(vext, vpairs, 6 + c)
        add_slots(ahead, vpairs, total, [4 - c, 4 + c])

    def between(h, carry):
        extra[h] = jnp.dot(ahead[h, 0], vpairs[h, 1], preferred_element_type=F32) + jnp.dot(
            ahead[h, 8], vpairs[h, 9], preferred_element_type=F32
        )
        return carry

    lax.fori_loop(0, HEADS, between, 0)
    inner_rows(total, extra, put_mixed)
    for k in (1, 2, 4):
        loads[k].wait()

    gain = gain_ref[...]

    def block_at(b):
        return pl.ds(pl.multiple_of(b * 128, 128), 128)

    def sums(stage, b, at):
        rows = block_at(b)
        hidden = gate_ref[rows, :].astype(F32) * mixed[rows, :]
        square = hidden * hidden
        inner = gain * grad_ref[rows, :].astype(F32) * hidden
        for k, v in ((0, square), (4, inner)):
            half = (v[:, :128] + v[:, 128:]).T
            chan_buf[stage, ch, pl.ds(k + at, 1), :] = jnp.sum(half, axis=0, keepdims=True)

    def inner_sums(i, carry):
        sums(0, i + 2, i)
        return carry

    def outer_sums(i, carry):
        sums(1, i + 4 * lax.div(i, 2), i)
        return carry

    def exchange(src_of, dst, send, recv, dev_of, order):
        return [
            pltpu.make_async_remote_copy(
                src_ref=src_of(j),
                dst_ref=dst,
                send_sem=send.at[j],
                recv_sem=recv.at[j],
                device_id=dev_of(j),
                device_id_type=MESH,
            )
            for j in order
        ]

    chan_copies = [
        exchange(
            lambda j, k=k: chan_buf.at[k, ch],
            chan_buf.at[k, ch],
            chan_send.at[k],
            chan_recv.at[k],
            chan_dev,
            far_first(chans),
        )
        for k in range(2)
    ]

    def scales(stage):
        for copy in chan_copies[stage]:
            copy.wait_recv()
        sums_all = chan_buf[stage, 0]
        for j in range(1, chans):
            sums_all = sums_all + chan_buf[stage, j]
        scale = lax.rsqrt(sums_all[0:4] / depth + EPS)
        row_scale[stage, 0:4, :] = scale
        row_scale[stage, 4:8, :] = scale * scale * sums_all[4:8] / depth

    gain_sum[...] = jnp.zeros((8, WIDTH), F32)

    def apply(stage, b, at):
        rows = block_at(b)

        def column(k):
            tall = jnp.broadcast_to(row_scale[stage, pl.ds(k + at, 1), :], (128, 128)).T
            return jnp.concatenate([tall, tall], axis=1)

        scale = column(0)
        pull = column(4)
        gate = gate_ref[rows, :].astype(F32)
        grad = grad_ref[rows, :].astype(F32)
        mix = mixed[rows, :]
        hidden = gate * mix
        scaled = hidden * scale
        normed_out[rows, :] = (scaled * gain).astype(BF16)
        hidden_grad = scale * (gain * grad - hidden * pull)
        gate_grad_out[rows, :] = (hidden_grad * mix).astype(BF16)
        mext[pl.ds(pl.multiple_of(ROWS + b * 128, 128), 128), :] = (hidden_grad * gate).astype(BF16)
        term = grad * scaled
        gain_sum[...] += jnp.sum(term.reshape(16, 8, WIDTH), axis=0)

    def apply_tile(t):
        def one(i, carry):
            if t in (1, 2):
                apply(0, 2 * t + i, 2 * t - 2 + i)
            else:
                apply(1, 2 * t + i, (0 if t == 0 else 2) + i)
            return carry

        lax.fori_loop(0, 2, one, 0)

    def send_next(*tiles):
        @pl.when(has_next)
        def _():
            for t in tiles:
                m_next[t].start()

    def send_prev(*tiles):
        @pl.when(has_prev)
        def _():
            for t in tiles:
                m_prev[t].start()

    lax.fori_loop(0, 4, inner_sums, 0)
    for copy in chan_copies[0]:
        copy.start()
    arrive(v_next, v_prev, [0], [3])
    make_pair(vext, vpairs, 0)
    make_pair(vext, vpairs, 10)
    add_slots(ahead, vpairs, total, [0, 8])
    outer_rows(total, put_mixed)
    lax.fori_loop(0, 4, outer_sums, 0)
    for copy in chan_copies[1]:
        copy.start()
    scales(0)
    apply_tile(1)
    send_prev(1)
    apply_tile(2)
    send_next(2, 1)
    send_prev(2)
    scales(1)
    apply_tile(0)
    apply_tile(3)

    for t in (4, 6):
        make_pair(mext, mpairs, t)

    def lag_terms(h, carry):
        local = jnp.concatenate([mpairs[h, 4], mpairs[h, 6]], axis=1)
        for s in range(SLOTS):
            window = jnp.concatenate([vpairs[h, s], vpairs[h, s + 2]], axis=1)
            cross = lax.dot_general(
                window, local, (((1,), (1,)), ((), ())), preferred_element_type=F32
            )
            at = (17 - 2 * s) * 128
            right = cross[0:128, 128:256]
            lag_sum[:, at + 128 : at + 256] = right if s == 0 else right + held
            lag_sum[:, at : at + 128] = cross[0:128, 0:128] + cross[128:256, 128:256]
            held = cross[128:256, 0:128]
        lag_sum[:, 0:128] = held
        eight = lag_sum[0:8, :]
        for g in range(1, 16):
            eight = eight + pltpu.roll(lag_sum[8 * g : 8 * g + 8, :], SPAN - 8 * g, 1)
        sub = lax.broadcasted_iota(jnp.int32, (8, SPAN), 0)
        for bit in (1, 2, 4):
            eight = jnp.where((sub & bit) != 0, pltpu.roll(eight, SPAN - bit, 1), eight)
        line = jnp.sum(eight, axis=0, keepdims=True)
        for b in range(16):
            row = h * 16 + b
            cut_src[lax.div(row, cut), pl.ds(lax.rem(row, cut), 1), :] = line[
                :, 128 + 128 * b : 256 + 128 * b
            ]
        return carry

    lax.fori_loop(0, HEADS, lag_terms, 0)
    gains = jnp.sum(gain_sum[...], axis=0, keepdims=True)
    gain_rows = jnp.concatenate([gains[:, :128], gains[:, 128:]], axis=0)
    for k in range(nz):
        cut_src[k, cut : cut + 2, :] = gain_rows

    cut_copies = exchange(
        lambda j: cut_src.at[z_of(j)], cut_buf.at[z], cut_send, cut_recv, z_dev, far_first(nz)
    )
    for copy in cut_copies:
        copy.start()
    send_next(3, 0)
    send_prev(0, 3)
    cut_buf[z] = cut_src[z]

    add_slots(behind, mpairs, total, [4], fresh=True)
    for copy in cut_copies:
        copy.wait_recv()
    part = cut_buf[0]
    for k in range(1, nz):
        part = part + cut_buf[k]
    all_buf[q] = part
    all_copies = exchange(
        lambda j: all_buf.at[q], all_buf.at[q], all_send, all_recv, q_dev, far_first_xy(nx, ny)
    )
    for copy in all_copies:
        copy.start()
    arrive(m_next, m_prev, [2, 1, 3], [1, 2, 0])
    for t in (1, 2, 3, 5, 7, 8, 9):
        make_pair(mext, mpairs, t)
    add_slots(behind, mpairs, total, [1, 2, 3])
    for copy in all_copies:
        copy.wait_recv()
    part = all_buf[0]
    for k in range(1, nq):
        part = part + all_buf[k]
    gather_buf[z] = part[0:cut] * (1.0 / math.sqrt(ROWS * nseq * 64))
    gather_copies = exchange(
        lambda j: gather_buf.at[z], gather_buf.at[z], gather_send, gather_recv, z_dev, far_first(nz)
    )
    for copy in gather_copies:
        copy.start()
    gains = jnp.concatenate([part[cut : cut + 1], part[cut + 1 : cut + 2]], axis=1)
    gain_grad_ref[...] = gains * (1.0 / math.sqrt(ROWS * nseq))
    add_slots(behind, mpairs, total, [5, 6, 7])
    arrive(m_next, m_prev, [0], [3])
    make_pair(mext, mpairs, 0)
    make_pair(mext, mpairs, 10)
    add_slots(behind, mpairs, total, [0, 8])

    def put_grad(p, hp, block):
        value_grad_out[tile_at(p), 128 * hp : 128 * hp + 128] = block.astype(BF16)

    all_rows(total, put_grad)
    for copy in gather_copies:
        copy.wait_recv()
    for row in range(64):
        h, b = divmod(row, 16)
        k, r = divmod(row, cut)
        taps_grad_ref[h : h + 1, 128 * b : 128 * b + 128] = gather_buf[k, r : r + 1, :]

    for copy in chan_copies[0] + chan_copies[1] + cut_copies + all_copies + gather_copies:
        copy.wait_send()

    @pl.when(has_next)
    def _():
        for t in range(4):
            v_next[t].wait_send()
            m_next[t].wait_send()

    @pl.when(has_prev)
    def _():
        for t in range(4):
            v_prev[t].wait_send()
            m_prev[t].wait_send()


def write_out(*refs):
    sources, targets, sem = refs[:5], refs[5:10], refs[10]
    copies = [
        pltpu.make_async_copy(source, target, sem.at[k])
        for k, (source, target) in enumerate(zip(sources, targets))
    ]
    for copy in copies:
        copy.start()
    for copy in copies:
        copy.wait()


def on_device(dims, chans, gate_acts, value_acts, taps, norm_gain, out_grad):
    ny, nz, nx = dims
    nq = ny * nx
    cut = 64 // nz
    block = jax.ShapeDtypeStruct((ROWS, WIDTH), BF16)
    hbm = pl.BlockSpec(memory_space=pltpu.HBM)
    vmem = pl.BlockSpec(memory_space=pltpu.VMEM)
    dma = pltpu.SemaphoreType.DMA
    call = pl.pallas_call(
        functools.partial(kernel_body, dims, chans),
        out_shape=(
            block,
            block,
            block,
            jax.ShapeDtypeStruct((HEADS, 2048), F32),
            jax.ShapeDtypeStruct((1, WIDTH), F32),
        ),
        in_specs=[hbm] * 5,
        out_specs=(vmem,) * 5,
        scratch_shapes=[
            pltpu.VMEM((3 * ROWS, WIDTH), BF16),
            pltpu.VMEM((3 * ROWS, WIDTH), BF16),
            pltpu.VMEM((ROWS, WIDTH), BF16),
            pltpu.VMEM((ROWS, WIDTH), BF16),
            pltpu.VMEM((HEADS, 2048), BF16),
            pltpu.VMEM((1, WIDTH), F32),
            pltpu.VMEM((HEADS, SLOTS, TILE, TILE), BF16),
            pltpu.VMEM((HEADS, SLOTS, TILE, TILE), BF16),
            pltpu.VMEM((HEADS, 11, TILE, 128), BF16),
            pltpu.VMEM((HEADS, 11, TILE, 128), BF16),
            pltpu.VMEM((HEADS, TILE, TILE), F32),
            pltpu.VMEM((HEADS, TILE, 128), F32),
            pltpu.VMEM((ROWS, WIDTH), F32),
            pltpu.VMEM((128, SPAN), F32),
            pltpu.VMEM((2, chans, 8, 128), F32),
            pltpu.VMEM((2, 8, 128), F32),
            pltpu.VMEM((8, WIDTH), F32),
            pltpu.VMEM((nz, cut + 2, 128), F32),
            pltpu.VMEM((nz, cut + 2, 128), F32),
            pltpu.VMEM((nq, cut + 2, 128), F32),
            pltpu.VMEM((nz, cut, 128), F32),
            dma((5,)),
            dma((2, 4)),
            dma((2, 4)),
            dma((2, 4)),
            dma((2, 4)),
            dma((2, chans)),
            dma((2, chans)),
            dma((nz,)),
            dma((nz,)),
            dma((nq,)),
            dma((nq,)),
            dma((nz,)),
            dma((nz,)),
        ],
        compiler_params=pltpu.CompilerParams(
            collective_id=0, has_side_effects=True, vmem_limit_bytes=52 * 1024 * 1024
        ),
        cost_estimate=pl.CostEstimate(
            flops=3_700_000_000, bytes_accessed=6_000_000, transcendentals=1024
        ),
        name="toeplitz_mix",
    )
    operands = (gate_acts, value_acts, taps, norm_gain.reshape(1, WIDTH), out_grad)
    results = call(*[pltpu.with_memory_space_constraint(v, pltpu.HBM) for v in operands])
    normed, gate_grad, value_grad, taps_grad, gain_grad = pl.pallas_call(
        write_out,
        out_shape=[jax.ShapeDtypeStruct(r.shape, r.dtype) for r in results],
        in_specs=[vmem] * 5,
        out_specs=[hbm] * 5,
        scratch_shapes=[dma((5,))],
        compiler_params=pltpu.CompilerParams(vmem_limit_bytes=8 * 1024 * 1024),
        name="write_out",
    )(*results)
    return normed, gate_grad, value_grad, taps_grad, gain_grad.reshape(WIDTH)


def solution(mesh, dims=(2, 8, 4)):
    placed = (P("seq", "chan"), P("seq", "chan"), P("chan", None), P("chan"), P("seq", "chan"))
    return jax.shard_map(
        functools.partial(on_device, dims, mesh.shape["chan"]),
        mesh=mesh,
        in_specs=placed,
        out_specs=(
            P("seq", "chan"),
            P("seq", "chan"),
            P("seq", "chan"),
            P("chan", None),
            P("chan"),
        ),
        check_vma=False,
    )
```
